32 devices in a mesh: shell: 2 (over y), row: 4 (over x, core), col: 4 (over z).
Axes of the slice: x: 2, y: 2, z: 4, core: 2. Of those that a mesh axis runs over, the one named last changes fastest.
Arguments:
- left_basis: bfloat16 [2, 1024, 1536], P(None, 'row', 'shell'), may hold values from -6 to 6
- right_basis: bfloat16 [2, 1536, 2048], P(None, 'shell', 'col'), may hold values from -0.15625 to 0.15625
- point_weight: float32 [1536], P('shell'), may hold values from 0.3 to 3
- shell_index: int32 [1536], P('shell'), may hold values from 0 to 11
- green_table: float32 [12, 2], replicated, may hold values from -4 to 4
- pivot_rows: int32 [512], replicated, may hold values from 0 to 1023, as said below
- diag_inverse: bfloat16 [2, 512, 512], replicated, may hold values from -0.005859375 to 0.005859375
Outputs:
- factored: float32 [2, 4, 2, 128, 2048], P(None, 'row', 'shell', None, 'col')
The draws below stay inside these ranges and needn't reach their ends.
Inputs may be any that keep to these rules, and one draw needn't show every extreme that they name: `pivot_rows`: 512 distinct matrix rows.
All inputs are finite; a program needn't handle non-finite values.
Results may differ from the reference program's by a relative error of at most 0.0056.
Values may be sent and summed in bfloat16 or wider, within the bound.
A program may use at most 128 MiB of HBM per device.

```python
import math
import jax
import jax.numpy as jnp
from jax import lax

W = 512
NK = 12
B = 128
MROWS = 1024
NCOLS = 2048
QTOT = 1536
N_SHELL = 2
N_ROW = 4


def draw_pivot_rows(key, part):
    first_key, second_key = jax.random.split(jax.random.fold_in(key, 7))
    middle_rows = jax.random.permutation(first_key, MROWS - 2)[:W - 2].astype(jnp.int32) + 1
    all_rows = jnp.concatenate([jnp.array([0, MROWS - 1], jnp.int32), middle_rows])
    shuffled = jax.random.permutation(second_key, W)
    return all_rows[shuffled].astype(jnp.int32)


def set_ends(entries, rng, least, top_value):
    longest = entries.shape.index(max(entries.shape))
    spots = []
    for shift in (0, 1):
        where = [jax.random.randint(jax.random.fold_in(rng, axis), (), 0, length) for axis, length in enumerate(entries.shape)]
        where[longest] = (where[longest] + shift) % entries.shape[longest]
        spots.append(tuple(where))
    return entries.at[spots[0]].set(least).at[spots[1]].set(top_value)


def block_scale(rng, dims, shards, least, high):
    def one(dim, blocks):
        steps = jax.random.uniform(jax.random.fold_in(jax.random.fold_in(rng, 6), dim), (blocks,), jnp.float32, least / len(shards), high / len(shards))
        return jnp.repeat(jnp.exp(steps), dims[dim] // blocks).reshape((-1,) + (1,) * (len(dims) - dim - 1))

    loudness = one(*shards[0])
    for cut in shards[1:]:
        loudness = loudness * one(*cut)
    return loudness


def normal_values(rng, dims, width, reach, cuts=(), kind=jnp.bfloat16):
    values = jax.random.normal(rng, dims, jnp.float32) * width
    if len(cuts) > 0:
        values = block_scale(rng, dims, cuts, -0.22, 0.18) * values
    return jnp.clip(values, min=-reach, max=reach).astype(kind)


def setup_inputs(seed: int = 0) -> dict:
    key_list = jax.random.split(jax.random.key(seed), 8)
    left_basis = normal_values(key_list[0], (2, MROWS, QTOT), 1.0, 6.0, ((1, 4), (2, 2)))
    right_basis = normal_values(key_list[1], (2, QTOT, NCOLS), QTOT ** -0.5, 0.15625, ((1, 2), (2, 4)))
    point_weight = jnp.clip(jnp.exp(math.log(3.0) - 2.3025851 * jax.random.uniform(key_list[2], (QTOT,), jnp.float32) ** block_scale(key_list[2], (QTOT,), ((0, 2),), -0.2, 0.2)), 0.3, 3.0)
    shell_index = set_ends(jax.random.randint(key_list[3], (QTOT,), 0, NK), jax.random.fold_in(key_list[3], 1), 0, NK - 1).astype(jnp.int32)
    green_table = normal_values(key_list[4], (NK, 2), 1.0, 4.0, (), jnp.float32)
    pivot_rows = draw_pivot_rows(jax.random.fold_in(key_list[7], 71), 0)
    diag_inverse = normal_values(key_list[6], (2, W, W), (0.5 / W), 0.005859375)
    return dict(left_basis=left_basis, right_basis=right_basis, point_weight=point_weight, shell_index=shell_index, green_table=green_table, pivot_rows=pivot_rows, diag_inverse=diag_inverse)


def reference(left_basis, right_basis, point_weight, shell_index, green_table, pivot_rows, diag_inverse):
    green_real = green_table[shell_index, 0]
    green_imag = green_table[shell_index, 1]
    weight_real = point_weight * green_real
    weight_imag = point_weight * green_imag
    basis_real = right_basis[0].astype(jnp.float32)
    basis_imag = right_basis[1].astype(jnp.float32)
    weighted_real = (weight_real[:, None] * basis_real - weight_imag[:, None] * basis_imag).astype(jnp.bfloat16)
    weighted_imag = (weight_real[:, None] * basis_imag + weight_imag[:, None] * basis_real).astype(jnp.bfloat16)
    coupling_real = jnp.dot(left_basis[0], weighted_real, preferred_element_type=jnp.float32) - jnp.dot(left_basis[1], weighted_imag, preferred_element_type=jnp.float32)
    coupling_imag = jnp.dot(left_basis[0], weighted_imag, preferred_element_type=jnp.float32) + jnp.dot(left_basis[1], weighted_real, preferred_element_type=jnp.float32)
    pivot_real = coupling_real[pivot_rows].astype(jnp.bfloat16)
    pivot_imag = coupling_imag[pivot_rows].astype(jnp.bfloat16)
    panel_real = coupling_real[:, :W]
    panel_imag = coupling_imag[:, :W]
    inverse_real = diag_inverse[0].astype(jnp.float32)
    inverse_imag = diag_inverse[1].astype(jnp.float32)
    highest = lax.Precision.HIGHEST
    mult_real = (jnp.dot(panel_real, inverse_real, precision=highest, preferred_element_type=jnp.float32) - jnp.dot(panel_imag, inverse_imag, precision=highest, preferred_element_type=jnp.float32)).astype(jnp.bfloat16)
    mult_imag = (jnp.dot(panel_real, inverse_imag, precision=highest, preferred_element_type=jnp.float32) + jnp.dot(panel_imag, inverse_real, precision=highest, preferred_element_type=jnp.float32)).astype(jnp.bfloat16)
    update_real = jnp.dot(mult_real, pivot_real, preferred_element_type=jnp.float32) - jnp.dot(mult_imag, pivot_imag, preferred_element_type=jnp.float32)
    update_imag = jnp.dot(mult_real, pivot_imag, preferred_element_type=jnp.float32) + jnp.dot(mult_imag, pivot_real, preferred_element_type=jnp.float32)
    updated = jnp.stack([coupling_real - update_real, coupling_imag - update_imag])
    return updated.reshape(2, N_ROW, N_SHELL, B, NCOLS)
```

```python
import functools
import jax
import jax.numpy as jnp
from jax import lax
from jax.experimental import pallas as pl
from jax.experimental.pallas import tpu as pltpu
from jax.sharding import PartitionSpec as P

MESH = pl.DeviceIdType.MESH
CORES = 2


def kernel(shells, rows, cols, chunk, left_ref, right_ref, point_ref, shell_ref, green_ref, pivot_ref,
           inverse_ref, out_ref, weights, stacked, part, outgoing, incoming, coupling, owned, mult,
           select, y_send, y_recv, x_send, x_recv, f_send, f_recv, m_send, m_recv):
    s = lax.axis_index("shell")
    r = lax.axis_index("row")
    col = lax.axis_index("col")
    chips = rows // CORES
    h = r // CORES
    core = lax.rem(r, CORES)
    sibling = h * CORES + (CORES - 1 - core)
    points = right_ref.shape[1]
    width = right_ref.shape[2]
    tile_rows = left_ref.shape[1]
    own = tile_rows // shells
    pieces = own // chunk
    half = mult.shape[2]
    halves = chunk // half
    bf16, f32 = jnp.bfloat16, jnp.float32

    barrier = pltpu.get_barrier_semaphore()

    def greet(**where):
        pl.semaphore_signal(barrier, inc=1, device_id=where, device_id_type=MESH)

    for o in range(1, shells):
        greet(shell=lax.rem(s + o, shells))
    for d in range(1, chips):
        greet(row=lax.rem(h + d, chips) * CORES + core)
    greet(row=sibling)

    @pl.when(col > 0)
    def _():
        greet(col=col - 1)

    @pl.when(col < cols - 1)
    def _():
        greet(col=col + 1)

    count = green_ref.shape[0]
    index = shell_ref[...].reshape(1, points)
    point = point_ref[...].reshape(1, points)
    hot = jnp.where(lax.broadcasted_iota(jnp.int32, (count, points), 0) == index, point, 0.0)
    table = jnp.concatenate(
        [jnp.broadcast_to(green_ref[:, i : i + 1], (count, 128)) for i in range(2)], axis=1
    )
    weights[...] = lax.dot_general(
        hot, table, (((0,), (0,)), ((), ())), precision=lax.Precision.HIGHEST, preferred_element_type=f32
    )

    def weigh(i, carry):
        at = pl.ds(pl.multiple_of(i * 128, 128), 128)
        low = pl.ds(pl.multiple_of(points + i * 128, 128), 128)
        w_real = jnp.concatenate([weights[at, :128]] * (width // 128), axis=1)
        w_imag = jnp.concatenate([weights[at, 128:]] * (width // 128), axis=1)
        b_real = right_ref[0, at, :].astype(f32)
        b_imag = right_ref[1, at, :].astype(f32)
        real = (w_real * b_real - w_imag * b_imag).astype(bf16)
        imag = (w_real * b_imag + w_imag * b_real).astype(bf16)
        stacked[at, :width] = real
        stacked[at, width:] = imag
        stacked[low, :width] = -imag
        stacked[low, width:] = real
        return carry

    lax.fori_loop(0, points // 128, weigh, 0)

    def span(first, size):
        return pl.ds(pl.multiple_of(first, size), size)

    def y_copy(o, j, c, group):
        at = span(group * own + c * chunk, chunk)
        return pltpu.make_async_remote_copy(
            src_ref=outgoing.at[at], dst_ref=incoming.at[o - 1, at],
            send_sem=y_send.at[o - 1, j, c], recv_sem=y_recv.at[o - 1, j, c],
            device_id={"shell": lax.rem(s + o, shells)}, device_id_type=MESH,
        )

    def x_copy(d, j, c, group, row):
        at = span(row * tile_rows + group * own + c * chunk, chunk)
        return pltpu.make_async_remote_copy(
            src_ref=coupling.at[at], dst_ref=coupling.at[at],
            send_sem=x_send.at[d - 1, j, c], recv_sem=x_recv.at[d - 1, j, c],
            device_id={"row": lax.rem(h + d, chips) * CORES + core}, device_id_type=MESH,
        )

    def f_copy(d, j, c, group, row):
        at = span(row * tile_rows + group * own + c * chunk, chunk)
        return pltpu.make_async_remote_copy(
            src_ref=coupling.at[at], dst_ref=coupling.at[at],
            send_sem=f_send.at[d, j, c], recv_sem=f_recv.at[d, j, c],
            device_id={"row": sibling}, device_id_type=MESH,
        )

    def m_copy(i):
        return pltpu.make_async_remote_copy(
            src_ref=mult.at[i], dst_ref=mult.at[i], send_sem=m_send.at[i], recv_sem=m_recv.at[i],
            device_id={"col": col + 1}, device_id_type=MESH,
        )

    for k in range(shells):
        group = lax.rem(s + 1 + k, shells)
        at = span(group * own, own)
        left = jnp.concatenate([left_ref[0, at, :], left_ref[1, at, :]], axis=1)
        term = jnp.dot(left, stacked[...], preferred_element_type=f32)
        part[at, :] = term
        outgoing[at, :] = term.astype(bf16)
        if k == 0:
            line = jnp.minimum(col, 1) + jnp.minimum(cols - 1 - col, 1)
            pl.semaphore_wait(barrier, shells - 1 + chips + line)

        for c in range(pieces):
            for o in range(1, shells):
                y_copy(o, (1 + k - o) % shells, c, group).start()

    pivots = pivot_ref[...].reshape(1, -1)

    def choose(i, carry):
        at = span(i * 128, 128)
        line = lax.broadcasted_iota(jnp.int32, (128, pivots.shape[1]), 0) + i * 128
        select[at, :] = jnp.where(line == pivots, 1.0, 0.0).astype(bf16)
        return carry

    lax.fori_loop(0, select.shape[0] // 128, choose, 0)

    def take_y(j, c):
        group = lax.rem(s + j, shells)
        at = span(group * own + c * chunk, chunk)
        total = part[at, :]
        for o in range(1, shells):
            y_copy(o, j, c, group).wait_recv()
            total = total + incoming[o - 1, at, :].astype(f32)
        coupling[span(r * tile_rows + group * own + c * chunk, chunk), :] = total.astype(bf16)
        if j == 0:
            owned[c * chunk : (c + 1) * chunk, :] = total
        for d in range(1, chips):
            x_copy(d, j, c, group, r).start()
        f_copy(0, j, c, group, r).start()
        if j == 0:

            @pl.when(col == 0)
            def _():
                panel = owned[c * chunk : (c + 1) * chunk, :]
                high = panel.astype(bf16)
                low = (panel - high.astype(f32)).astype(bf16)
                four = jnp.concatenate(
                    [high[:, :width], low[:, :width], high[:, width:], low[:, width:]], axis=0
                )
                by_real = jnp.dot(four, inverse_ref[0], preferred_element_type=f32)
                by_imag = jnp.dot(four, inverse_ref[1], preferred_element_type=f32)

                def pick(product, first):
                    return product[first : first + chunk] + product[first + chunk : first + 2 * chunk]

                m_real = (pick(by_real, 0) - pick(by_imag, 2 * chunk)).astype(bf16)
                m_imag = (pick(by_imag, 0) + pick(by_real, 2 * chunk)).astype(bf16)
                for p in range(halves):
                    i = c * halves + p
                    mult[i, 0] = m_real[p * half : (p + 1) * half]
                    mult[i, 1] = m_imag[p * half : (p + 1) * half]
                    if cols > 1:
                        m_copy(i).start()

    def take_x(j, c):
        group = lax.rem(s + j, shells)
        for d in range(1, chips):
            row = lax.rem(h - d + chips, chips) * CORES + core
            x_copy(d, j, c, group, row).wait_recv()
            f_copy(d, j, c, group, row).start()

    def pass_mult(i):
        @pl.when((col > 0) & (col < cols - 1))
        def _():
            m_copy(i).wait_recv()
            m_copy(i).start()

    steps = [(j, c) for j in range(shells) for c in range(pieces)]
    passes = pieces * halves
    done = 0
    for n, (j, c) in enumerate(steps):
        take_y(j, c)
        if n >= 1:
            take_x(*steps[n - 1])
        if n >= len(steps) // 2 and done < passes:
            pass_mult(done)
            done += 1
    if done < passes:
        pass_mult(done)
        done += 1
    take_x(*steps[-1])
    while done < passes:
        pass_mult(done)
        done += 1

    for j, c in steps:
        group = lax.rem(s + j, shells)
        f_copy(0, j, c, group, sibling).wait_recv()
        for d in range(1, chips):
            row = lax.rem(h - d + chips, chips) * CORES + (CORES - 1 - core)
            f_copy(d, j, c, group, row).wait_recv()

    @pl.when((col == cols - 1) & (col > 0))
    def _():
        for i in range(passes):
            m_copy(i).wait_recv()

    factors = jnp.concatenate(
        [mult[i, p] for p in range(2) for i in range(passes)], axis=0
    )
    spread = lax.dot_general(
        factors, select[...], (((1,), (1,)), ((), ())), preferred_element_type=f32
    ).astype(bf16)
    product = jnp.dot(spread, coupling[...], preferred_element_type=f32)
    out_ref[0, 0, 0] = owned[:, :width] - (product[:own, :width] - product[own:, width:])
    out_ref[1, 0, 0] = owned[:, width:] - (product[:own, width:] + product[own:, :width])

    for j, c in steps:
        group = lax.rem(s + j, shells)
        for o in range(1, shells):
            y_copy(o, j, c, group).wait_send()
        f_copy(0, j, c, group, r).wait_send()
        for d in range(1, chips):
            x_copy(d, j, c, group, r).wait_send()
            f_copy(d, j, c, group, lax.rem(h - d + chips, chips) * CORES + core).wait_send()

    @pl.when(col < cols - 1)
    def _():
        for i in range(passes):
            m_copy(i).wait_send()


def body(sizes, left_basis, right_basis, point_weight, shell_index, green_table, pivot_rows, diag_inverse):
    shells, rows, cols = sizes
    chips = rows // CORES
    tile_rows, points = left_basis.shape[1:]
    width = right_basis.shape[2]
    own = tile_rows // shells
    chunk = own // 2
    half = chunk // 2
    pieces = own // chunk
    all_rows = rows * tile_rows
    bf16, f32 = jnp.bfloat16, jnp.float32
    vmem = pl.BlockSpec(memory_space=pltpu.VMEM)
    sems = pltpu.SemaphoreType.DMA
    return pl.pallas_call(
        functools.partial(kernel, shells, rows, cols, chunk),
        out_shape=jax.ShapeDtypeStruct((2, 1, 1, own, width), f32),
        in_specs=[vmem] * 7,
        out_specs=vmem,
        scratch_shapes=[
            pltpu.VMEM((points, 256), f32),
            pltpu.VMEM((2 * points, 2 * width), bf16),
            pltpu.VMEM((tile_rows, 2 * width), f32),
            pltpu.VMEM((tile_rows, 2 * width), bf16),
            pltpu.VMEM((max(shells - 1, 1), tile_rows, 2 * width), bf16),
            pltpu.VMEM((all_rows, 2 * width), bf16),
            pltpu.VMEM((own, 2 * width), f32),
            pltpu.VMEM((own // half, 2, half, width), bf16),
            pltpu.VMEM((all_rows, pivot_rows.shape[0]), bf16),
            sems((max(shells - 1, 1), shells, pieces)),
            sems((max(shells - 1, 1), shells, pieces)),
            sems((max(chips - 1, 1), shells, pieces)),
            sems((max(chips - 1, 1), shells, pieces)),
            sems((chips, shells, pieces)),
            sems((chips, shells, pieces)),
            sems((own // half,)),
            sems((own // half,)),
        ],
        compiler_params=pltpu.CompilerParams(
            collective_id=0, has_side_effects=True, vmem_limit_bytes=56 * 2**20
        ),
        cost_estimate=pl.CostEstimate(
            flops=2 * tile_rows * 2 * points * 2 * width + 4 * own * all_rows * 2 * width,
            bytes_accessed=8 * 2**20,
            transcendentals=0,
        ),
    )(left_basis, right_basis, point_weight, shell_index, green_table, pivot_rows, diag_inverse)


def solution(mesh):
    sizes = tuple(mesh.shape[name] for name in ("shell", "row", "col"))
    return jax.shard_map(
        functools.partial(body, sizes),
        mesh=mesh,
        in_specs=(
            P(None, "row", "shell"),
            P(None, "shell", "col"),
            P("shell"),
            P("shell"),
            P(),
            P(),
            P(),
        ),
        out_specs=P(None, "row", "shell", None, "col"),
        check_vma=False,
    )
```

```python
import functools
import math
import jax
import jax.numpy as jnp
from jax import lax
from jax.experimental import pallas as pl
from jax.experimental.pallas import tpu as pltpu
from jax.sharding import PartitionSpec as P

MESH = pl.DeviceIdType.MESH
CORES = 2


def kernel(shells, rows, cols, chunk, left_hbm, right_hbm, point_hbm, shell_hbm, green_hbm, pivot_hbm,
           inverse_hbm, out_ref, left_ref, right_ref, inverse_ref, point_ref, shell_ref, green_ref, pivot_ref, weights, weighted, product, part,
           outgoing, incoming, coupling, owned, mult, select, spread, in_sem, y_send, y_recv, x_send,
           x_recv, f_send, f_recv, m_send, m_recv):
    s = lax.axis_index("shell")
    r = lax.axis_index("row")
    col = lax.axis_index("col")
    chips = rows // CORES
    h = r // CORES
    core = lax.rem(r, CORES)
    sibling = h * CORES + (CORES - 1 - core)
    points = right_ref.shape[1]
    width = right_ref.shape[2]
    tile_rows = left_ref.shape[1]
    own = tile_rows // shells
    pieces = own // chunk
    half = mult.shape[2]
    batch = 2 * chunk
    halves = batch // half
    bf16, f32 = jnp.bfloat16, jnp.float32

    slab = 256
    slabs = points // slab
    right_in = [
        pltpu.make_async_copy(
            right_hbm.at[:, pl.ds(b * slab, slab)], right_ref.at[:, pl.ds(b * slab, slab)], in_sem.at[b]
        )
        for b in range(slabs)
    ]
    left_in = pltpu.make_async_copy(left_hbm, left_ref, in_sem.at[slabs])
    inverse_in = pltpu.make_async_copy(inverse_hbm, inverse_ref, in_sem.at[slabs + 1])
    small_in = [
        pltpu.make_async_copy(source, target, in_sem.at[slabs + 2 + i])
        for i, (source, target) in enumerate([
            (point_hbm, point_ref), (shell_hbm, shell_ref), (green_hbm, green_ref), (pivot_hbm, pivot_ref)
        ])
    ]
    for copy in small_in[:3]:
        copy.start()
    right_in[0].start()
    left_in.start()
    for copy in right_in[1:]:
        copy.start()
    small_in[3].start()

    @pl.when(col == 0)
    def _():
        inverse_in.start()

    barrier = pltpu.get_barrier_semaphore()

    def greet(**where):
        pl.semaphore_signal(barrier, inc=1, device_id=where, device_id_type=MESH)

    for o in range(1, shells):
        greet(shell=lax.rem(s + o, shells))
    for d in range(1, chips):
        greet(row=lax.rem(h + d, chips) * CORES + core)
    greet(row=sibling)

    @pl.when(col > 0)
    def _():
        greet(col=col - 1)

    @pl.when(col < cols - 1)
    def _():
        greet(col=col + 1)

    for copy in small_in[:3]:
        copy.wait()
    count = green_ref.shape[1]
    index = shell_ref[...].reshape(1, points)
    point = point_ref[...].reshape(1, points)
    hot = jnp.where(lax.broadcasted_iota(jnp.int32, (count, points), 0) == index, point, 0.0)
    square = (count, count)
    same = lax.broadcasted_iota(jnp.int32, square, 0) == lax.broadcasted_iota(jnp.int32, square, 1)
    table = jnp.concatenate(
        [
            jnp.broadcast_to(
                jnp.sum(
                    jnp.where(same, jnp.broadcast_to(green_ref[i : i + 1, :], square), 0.0),
                    axis=1, keepdims=True,
                ),
                (count, 128),
            )
            for i in range(2)
        ],
        axis=1,
    )
    weights[...] = lax.dot_general(
        hot, table, (((0,), (0,)), ((), ())), precision=lax.Precision.HIGHEST, preferred_element_type=f32
    )

    def span(first, size):
        return pl.ds(pl.multiple_of(first, size), size)

    def y_copy(o, j, c, group):
        at = span(group * own + c * chunk, chunk)
        return pltpu.make_async_remote_copy(
            src_ref=outgoing.at[at], dst_ref=incoming.at[o - 1, at],
            send_sem=y_send.at[o - 1, j, c], recv_sem=y_recv.at[o - 1, j, c],
            device_id={"shell": lax.rem(s + o, shells)}, device_id_type=MESH,
        )

    def x_copy(d, j, c, group, row):
        at = span(row * tile_rows + group * own + c * chunk, chunk)
        return pltpu.make_async_remote_copy(
            src_ref=coupling.at[at], dst_ref=coupling.at[at],
            send_sem=x_send.at[d - 1, j, c], recv_sem=x_recv.at[d - 1, j, c],
            device_id={"row": lax.rem(h + d, chips) * CORES + core}, device_id_type=MESH,
        )

    def f_copy(d, j, c, group, row):
        at = span(row * tile_rows + group * own + c * chunk, chunk)
        return pltpu.make_async_remote_copy(
            src_ref=coupling.at[at], dst_ref=coupling.at[at],
            send_sem=f_send.at[d, j, c], recv_sem=f_recv.at[d, j, c],
            device_id={"row": sibling}, device_id_type=MESH,
        )

    def m_copy(i):
        return pltpu.make_async_remote_copy(
            src_ref=mult.at[i], dst_ref=mult.at[i], send_sem=m_send.at[i], recv_sem=m_recv.at[i],
            device_id={"col": col + 1}, device_id_type=MESH,
        )

    def left_rows(group, at):
        rows_at = span(group * own, own)
        return jnp.concatenate([left_ref[0, rows_at, at], left_ref[1, rows_at, at]], axis=0)

    def combine(four):
        real = four[:own, :width] - four[own:, width:]
        return real, four[:own, width:] + four[own:, :width]

    first = lax.rem(s + 1, shells)
    for b in range(slabs):
        at = pl.ds(b * slab, slab)
        right_in[b].wait()
        w_real = jnp.concatenate([weights[at, :128]] * (width // 128), axis=1)
        w_imag = jnp.concatenate([weights[at, 128:]] * (width // 128), axis=1)
        b_real = right_ref[0, at, :].astype(f32)
        b_imag = right_ref[1, at, :].astype(f32)
        weighted[at, :width] = (w_real * b_real - w_imag * b_imag).astype(bf16)
        weighted[at, width:] = (w_real * b_imag + w_imag * b_real).astype(bf16)
        if b == 0:
            left_in.wait()
        term = jnp.dot(left_rows(first, at), weighted[at, :], preferred_element_type=f32)
        product[...] = term if b == 0 else product[...] + term

    for k in range(shells):
        group = lax.rem(s + 1 + k, shells)
        at = span(group * own, own)
        if k > 0:
            product[...] = jnp.dot(
                left_rows(group, pl.ds(0, points)), weighted[...], preferred_element_type=f32
            )
        real, imag = combine(product[...])
        part[at, :width] = real
        part[at, width:] = imag
        outgoing[at, :width] = real.astype(bf16)
        outgoing[at, width:] = imag.astype(bf16)
        if k == 0:
            line = jnp.minimum(col, 1) + jnp.minimum(cols - 1 - col, 1)
            pl.semaphore_wait(barrier, shells - 1 + chips + line)

        for c in range(pieces):
            for o in range(1, shells):
                y_copy(o, (1 + k - o) % shells, c, group).start()

    small_in[3].wait()
    pivots = pivot_ref[...].reshape(1, -1)

    def choose(i, carry):
        at = span(i * 128, 128)
        line = lax.broadcasted_iota(jnp.int32, (128, pivots.shape[1]), 0) + i * 128
        select[at, :] = jnp.where(line == pivots, 1.0, 0.0).astype(bf16)
        return carry

    lax.fori_loop(0, select.shape[0] // 128, choose, 0)

    def take_y(j, c):
        group = lax.rem(s + j, shells)
        at = span(group * own + c * chunk, chunk)
        total = part[at, :]
        for o in range(1, shells):
            y_copy(o, j, c, group).wait_recv()
            total = total + incoming[o - 1, at, :].astype(f32)
        coupling[span(r * tile_rows + group * own + c * chunk, chunk), :] = total.astype(bf16)
        if j == 0:
            owned[c * chunk : (c + 1) * chunk, :] = total
        for d in range(1, chips):
            x_copy(d, j, c, group, r).start()
        f_copy(0, j, c, group, r).start()
        if j == 0 and (c + 1) * chunk % batch == 0:

            @pl.when(col == 0)
            def _():
                base = (c + 1) * chunk - batch
                if base == 0:
                    inverse_in.wait()
                panel = owned[base : base + batch, :]
                high = panel.astype(bf16)
                low = (panel - high.astype(f32)).astype(bf16)
                four = jnp.concatenate(
                    [high[:, :width], low[:, :width], high[:, width:], low[:, width:]], axis=0
                )
                by_real = jnp.dot(four, inverse_ref[0], preferred_element_type=f32)
                by_imag = jnp.dot(four, inverse_ref[1], preferred_element_type=f32)

                def pick(value, at):
                    return value[at : at + batch] + value[at + batch : at + 2 * batch]

                m_real = (pick(by_real, 0) - pick(by_imag, 2 * batch)).astype(bf16)
                m_imag = (pick(by_imag, 0) + pick(by_real, 2 * batch)).astype(bf16)
                for p in range(halves):
                    i = base // half + p
                    mult[i, 0] = m_real[p * half : (p + 1) * half]
                    mult[i, 1] = m_imag[p * half : (p + 1) * half]
                    if cols > 1:
                        m_copy(i).start()

    def take_x(j, c):
        group = lax.rem(s + j, shells)
        for d in range(1, chips):
            row = lax.rem(h - d + chips, chips) * CORES + core
            x_copy(d, j, c, group, row).wait_recv()
            f_copy(d, j, c, group, row).start()

    def pass_mult(i):
        @pl.when((col > 0) & (col < cols - 1))
        def _():
            m_copy(i).wait_recv()
            m_copy(i).start()

    def take_sibling(d, j, c):
        group = lax.rem(s + j, shells)
        row = lax.rem(h - d + chips, chips) * CORES + (CORES - 1 - core)
        f_copy(d, j, c, group, row).wait_recv()

    steps = [(j, c) for j in range(shells) for c in range(pieces)]
    passes = own // half
    done = 0
    for n, (j, c) in enumerate(steps):
        take_y(j, c)
        if n >= pieces - 1 and done < passes:
            pass_mult(done)
            done += 1
        if n >= 2:
            take_x(*steps[n - 2])
    for i in range(done, passes):
        pass_mult(i)
    take_x(*steps[-2])

    @pl.when((col == cols - 1) & (col > 0))
    def _():
        for i in range(passes):
            m_copy(i).wait_recv()

    factors = jnp.concatenate([mult[i, p] for p in range(2) for i in range(passes)], axis=0)
    spread[...] = lax.dot_general(
        factors, select[...], (((1,), (1,)), ((), ())), preferred_element_type=f32
    ).astype(bf16)
    for j, c in steps:
        take_sibling(0, j, c)
    near = span(h * CORES * tile_rows, CORES * tile_rows)
    product[...] = jnp.dot(spread[:, near], coupling[near, :], preferred_element_type=f32)
    take_x(*steps[-1])
    for j in range(shells):
        group = lax.rem(s + j, shells)
        for d in range(1, chips):
            for c in range(pieces):
                take_sibling(d, j, c)
            first_row = lax.rem(h - d + chips, chips) * CORES * tile_rows + group * own
            spots = [span(first_row + i * tile_rows, own) for i in range(CORES)]
            product[...] += jnp.dot(
                jnp.concatenate([spread[:, at] for at in spots], axis=1),
                jnp.concatenate([coupling[at, :] for at in spots], axis=0),
                preferred_element_type=f32,
            )
    real, imag = combine(product[...])
    out_ref[0, 0, 0] = owned[:, :width] - real
    out_ref[1, 0, 0] = owned[:, width:] - imag

    for j, c in steps:
        group = lax.rem(s + j, shells)
        for o in range(1, shells):
            y_copy(o, j, c, group).wait_send()
        f_copy(0, j, c, group, r).wait_send()
        for d in range(1, chips):
            x_copy(d, j, c, group, r).wait_send()
            f_copy(d, j, c, group, lax.rem(h - d + chips, chips) * CORES + core).wait_send()

    @pl.when(col < cols - 1)
    def _():
        for i in range(passes):
            m_copy(i).wait_send()


def body(sizes, left_basis, right_basis, point_weight, shell_index, green_table, pivot_rows, diag_inverse):
    shells, rows, cols = sizes
    chips = rows // CORES
    tile_rows, points = left_basis.shape[1:]
    width = right_basis.shape[2]
    own = tile_rows // shells
    chunk = own // 4
    half = chunk
    pieces = own // chunk
    all_rows = rows * tile_rows
    bf16, f32 = jnp.bfloat16, jnp.float32
    vmem = pl.BlockSpec(memory_space=pltpu.VMEM)
    sems = pltpu.SemaphoreType.DMA
    buffers = [
        ((2, tile_rows, points), bf16),
        ((2, points, width), bf16),
        (diag_inverse.shape, bf16),
        (point_weight.shape, f32),
        (shell_index.shape, jnp.int32),
        (green_table.shape[::-1], f32),
        (pivot_rows.shape, jnp.int32),
        ((points, 256), f32),
        ((points, 2 * width), bf16),
        ((2 * own, 2 * width), f32),
        ((tile_rows, 2 * width), f32),
        ((tile_rows, 2 * width), bf16),
        ((max(shells - 1, 1), tile_rows, 2 * width), bf16),
        ((all_rows, 2 * width), bf16),
        ((own, 2 * width), f32),
        ((own // half, 2, half, width), bf16),
        ((all_rows, pivot_rows.shape[0]), bf16),
        ((2 * own, all_rows), bf16),
    ]
    held = sum(math.prod(shape) * jnp.dtype(kind).itemsize for shape, kind in buffers)
    return pl.pallas_call(
        functools.partial(kernel, shells, rows, cols, chunk),
        out_shape=jax.ShapeDtypeStruct((2, 1, 1, own, width), f32),
        in_specs=[pl.BlockSpec(memory_space=pltpu.HBM)] * 7,
        out_specs=vmem,
        scratch_shapes=[pltpu.VMEM(shape, kind) for shape, kind in buffers] + [
            sems((points // 256 + 6,)),
            sems((max(shells - 1, 1), shells, pieces)),
            sems((max(shells - 1, 1), shells, pieces)),
            sems((max(chips - 1, 1), shells, pieces)),
            sems((max(chips - 1, 1), shells, pieces)),
            sems((chips, shells, pieces)),
            sems((chips, shells, pieces)),
            sems((own // half,)),
            sems((own // half,)),
        ],
        compiler_params=pltpu.CompilerParams(
            collective_id=0, has_side_effects=True, vmem_limit_bytes=56 * 2**20
        ),
        cost_estimate=pl.CostEstimate(
            flops=2 * tile_rows * 2 * points * 2 * width + 4 * own * all_rows * 2 * width,
            bytes_accessed=8 * 2**20,
            transcendentals=0,
        ),
    )(left_basis, right_basis, point_weight, shell_index, green_table.T, pivot_rows, diag_inverse)


def solution(mesh):
    sizes = tuple(mesh.shape[name] for name in ("shell", "row", "col"))
    return jax.shard_map(
        functools.partial(body, sizes),
        mesh=mesh,
        in_specs=(
            P(None, "row", "shell"),
            P(None, "shell", "col"),
            P("shell"),
            P("shell"),
            P(),
            P(),
            P(),
        ),
        out_specs=P(None, "row", "shell", None, "col"),
        check_vma=False,
    )
```

```python
import functools
import math
import jax
import jax.numpy as jnp
from jax import lax
from jax.experimental import pallas as pl
from jax.experimental.pallas import tpu as pltpu
from jax.sharding import PartitionSpec as P

MESH = pl.DeviceIdType.MESH
CORES = 2


def kernel(shells, rows, cols, chunk, left_hbm, right_hbm, point_hbm, shell_hbm, green_hbm, pivot_hbm,
           inverse_hbm, out_ref, left_ref, right_ref, inverse_ref, point_ref, shell_ref, green_ref, pivot_ref, weights, weighted, product, part,
           outgoing, incoming, coupling, owned, mult, select, spread, in_sem, y_send, y_recv, x_send,
           x_recv, f_send, f_recv, m_send, m_recv):
    s = lax.axis_index("shell")
    r = lax.axis_index("row")
    col = lax.axis_index("col")
    chips = rows // CORES
    h = r // CORES
    core = lax.rem(r, CORES)
    sibling = h * CORES + (CORES - 1 - core)
    points = right_ref.shape[1]
    width = right_ref.shape[2]
    tile_rows = left_ref.shape[1]
    own = tile_rows // shells
    pieces = own // chunk
    half = mult.shape[2]
    batch = 2 * chunk
    halves = batch // half
    bf16, f32 = jnp.bfloat16, jnp.float32

    slab = 256
    slabs = points // slab
    right_in = [
        pltpu.make_async_copy(
            right_hbm.at[:, pl.ds(b * slab, slab)], right_ref.at[:, pl.ds(b * slab, slab)], in_sem.at[b]
        )
        for b in range(slabs)
    ]
    left_in = pltpu.make_async_copy(left_hbm, left_ref, in_sem.at[slabs])
    inverse_in = pltpu.make_async_copy(inverse_hbm, inverse_ref, in_sem.at[slabs + 1])
    small_in = [
        pltpu.make_async_copy(source, target, in_sem.at[slabs + 2 + i])
        for i, (source, target) in enumerate([
            (point_hbm, point_ref), (shell_hbm, shell_ref), (green_hbm, green_ref), (pivot_hbm, pivot_ref)
        ])
    ]
    for copy in small_in[:3]:
        copy.start()
    right_in[0].start()
    left_in.start()
    for copy in right_in[1:]:
        copy.start()
    small_in[3].start()

    @pl.when(col == 0)
    def _():
        inverse_in.start()

    barrier = pltpu.get_barrier_semaphore()

    def greet(**where):
        pl.semaphore_signal(barrier, inc=1, device_id=where, device_id_type=MESH)

    for o in range(1, shells):
        greet(shell=lax.rem(s + o, shells))
    for d in range(1, chips):
        greet(row=lax.rem(h + d, chips) * CORES + core)
    greet(row=sibling)

    @pl.when(col > 0)
    def _():
        greet(col=col - 1)

    @pl.when(col < cols - 1)
    def _():
        greet(col=col + 1)

    for copy in small_in[:3]:
        copy.wait()
    count = green_ref.shape[1]
    padded = -(-count // 16) * 16
    index = shell_ref[...].reshape(1, points)
    match = lax.broadcasted_iota(jnp.int32, (padded, points), 0) == index

    def pieces_of(value):
        first = value.astype(bf16).astype(f32)
        second = (value - first).astype(bf16).astype(f32)
        return first, second, value - first - second

    hot = [jnp.where(match, piece, 0.0).astype(bf16) for piece in pieces_of(point_ref[...].reshape(1, points))]
    square = (padded, count)
    same = lax.broadcasted_iota(jnp.int32, square, 0) == lax.broadcasted_iota(jnp.int32, square, 1)
    table = jnp.concatenate(
        [
            jnp.broadcast_to(
                jnp.sum(
                    jnp.where(same, jnp.broadcast_to(green_ref[i : i + 1, :], square), 0.0),
                    axis=1, keepdims=True,
                ),
                (padded, 128),
            )
            for i in range(2)
        ],
        axis=1,
    )
    green = [piece.astype(bf16) for piece in pieces_of(table)]
    pairs = [(i, j) for i in range(3) for j in range(3 - i)]
    weights[...] = lax.dot_general(
        jnp.concatenate([hot[i] for i, _ in pairs], axis=0),
        jnp.concatenate([green[j] for _, j in pairs], axis=0),
        (((0,), (0,)), ((), ())),
        preferred_element_type=f32,
    )

    def span(first, size):
        return pl.ds(pl.multiple_of(first, size), size)

    def y_copy(o, j, c, group):
        at = span(group * own + c * chunk, chunk)
        return pltpu.make_async_remote_copy(
            src_ref=outgoing.at[at], dst_ref=incoming.at[o - 1, at],
            send_sem=y_send.at[o - 1, j, c], recv_sem=y_recv.at[o - 1, j, c],
            device_id={"shell": lax.rem(s + o, shells)}, device_id_type=MESH,
        )

    def x_copy(d, j, c, group, row):
        at = span(row * tile_rows + group * own + c * chunk, chunk)
        return pltpu.make_async_remote_copy(
            src_ref=coupling.at[at], dst_ref=coupling.at[at],
            send_sem=x_send.at[d - 1, j, c], recv_sem=x_recv.at[d - 1, j, c],
            device_id={"row": lax.rem(h + d, chips) * CORES + core}, device_id_type=MESH,
        )

    def f_copy(d, j, c, group, row):
        at = span(row * tile_rows + group * own + c * chunk, chunk)
        return pltpu.make_async_remote_copy(
            src_ref=coupling.at[at], dst_ref=coupling.at[at],
            send_sem=f_send.at[d, j, c], recv_sem=f_recv.at[d, j, c],
            device_id={"row": sibling}, device_id_type=MESH,
        )

    def m_copy(i):
        return pltpu.make_async_remote_copy(
            src_ref=mult.at[i], dst_ref=mult.at[i], send_sem=m_send.at[i], recv_sem=m_recv.at[i],
            device_id={"col": col + 1}, device_id_type=MESH,
        )

    def left_rows(group, at):
        rows_at = span(group * own, own)
        return jnp.concatenate([left_ref[0, rows_at, at], left_ref[1, rows_at, at]], axis=0)

    def combine(four):
        real = four[:own, :width] - four[own:, width:]
        return real, four[:own, width:] + four[own:, :width]

    first = lax.rem(s + 1, shells)
    for b in range(slabs):
        at = pl.ds(b * slab, slab)
        right_in[b].wait()
        w_real = jnp.concatenate([weights[at, :128]] * (width // 128), axis=1)
        w_imag = jnp.concatenate([weights[at, 128:]] * (width // 128), axis=1)
        b_real = right_ref[0, at, :].astype(f32)
        b_imag = right_ref[1, at, :].astype(f32)
        weighted[at, :width] = (w_real * b_real - w_imag * b_imag).astype(bf16)
        weighted[at, width:] = (w_real * b_imag + w_imag * b_real).astype(bf16)
        if b == 0:
            left_in.wait()
        term = jnp.dot(left_rows(first, at), weighted[at, :], preferred_element_type=f32)
        product[...] = term if b == 0 else product[...] + term

    for k in range(shells):
        group = lax.rem(s + 1 + k, shells)
        at = span(group * own, own)
        if k > 0:
            product[...] = jnp.dot(
                left_rows(group, pl.ds(0, points)), weighted[...], preferred_element_type=f32
            )
        real, imag = combine(product[...])
        part[at, :width] = real
        part[at, width:] = imag
        outgoing[at, :width] = real.astype(bf16)
        outgoing[at, width:] = imag.astype(bf16)
        if k == 0:
            line = jnp.minimum(col, 1) + jnp.minimum(cols - 1 - col, 1)
            pl.semaphore_wait(barrier, shells - 1 + chips + line)

        for c in range(pieces):
            for o in range(1, shells):
                y_copy(o, (1 + k - o) % shells, c, group).start()

    small_in[3].wait()
    pivots = pivot_ref[...].reshape(1, -1)

    def choose(i, carry):
        at = span(i * 128, 128)
        line = lax.broadcasted_iota(jnp.int32, (128, pivots.shape[1]), 0) + i * 128
        select[at, :] = jnp.where(line == pivots, 1.0, 0.0).astype(bf16)
        return carry

    lax.fori_loop(0, select.shape[0] // 128, choose, 0)

    def take_y(j, c):
        group = lax.rem(s + j, shells)
        at = span(group * own + c * chunk, chunk)
        total = part[at, :]
        for o in range(1, shells):
            y_copy(o, j, c, group).wait_recv()
            total = total + incoming[o - 1, at, :].astype(f32)
        coupling[span(r * tile_rows + group * own + c * chunk, chunk), :] = total.astype(bf16)
        if j == 0:
            owned[c * chunk : (c + 1) * chunk, :] = total
        for d in range(1, chips):
            x_copy(d, j, c, group, r).start()
        f_copy(0, j, c, group, r).start()
        if j == 0 and (c + 1) * chunk % batch == 0:

            @pl.when(col == 0)
            def _():
                base = (c + 1) * chunk - batch
                if base == 0:
                    inverse_in.wait()
                panel = owned[base : base + batch, :]
                high = panel.astype(bf16)
                low = (panel - high.astype(f32)).astype(bf16)
                four = jnp.concatenate(
                    [high[:, :width], low[:, :width], high[:, width:], low[:, width:]], axis=0
                )
                by_real = jnp.dot(four, inverse_ref[0], preferred_element_type=f32)
                by_imag = jnp.dot(four, inverse_ref[1], preferred_element_type=f32)

                def pick(value, at):
                    return value[at : at + batch] + value[at + batch : at + 2 * batch]

                m_real = (pick(by_real, 0) - pick(by_imag, 2 * batch)).astype(bf16)
                m_imag = (pick(by_imag, 0) + pick(by_real, 2 * batch)).astype(bf16)
                for p in range(halves):
                    i = base // half + p
                    mult[i, 0] = m_real[p * half : (p + 1) * half]
                    mult[i, 1] = m_imag[p * half : (p + 1) * half]
                    if cols > 1:
                        m_copy(i).start()

    def take_x(j, c):
        group = lax.rem(s + j, shells)
        for d in range(1, chips):
            row = lax.rem(h - d + chips, chips) * CORES + core
            x_copy(d, j, c, group, row).wait_recv()
            f_copy(d, j, c, group, row).start()

    def pass_mult(i):
        @pl.when((col > 0) & (col < cols - 1))
        def _():
            m_copy(i).wait_recv()
            m_copy(i).start()

    def take_sibling(d, j, c):
        group = lax.rem(s + j, shells)
        row = lax.rem(h - d + chips, chips) * CORES + (CORES - 1 - core)
        f_copy(d, j, c, group, row).wait_recv()

    steps = [(j, c) for j in range(shells) for c in range(pieces)]
    passes = own // half
    done = 0
    for n, (j, c) in enumerate(steps):
        take_y(j, c)
        if n >= pieces - 1 and done < passes:
            pass_mult(done)
            done += 1
        if n >= 2:
            take_x(*steps[n - 2])
    for i in range(done, passes):
        pass_mult(i)
    take_x(*steps[-2])

    @pl.when((col == cols - 1) & (col > 0))
    def _():
        for i in range(passes):
            m_copy(i).wait_recv()

    factors = jnp.concatenate([mult[i, p] for p in range(2) for i in range(passes)], axis=0)
    spread[...] = lax.dot_general(
        factors, select[...], (((1,), (1,)), ((), ())), preferred_element_type=f32
    ).astype(bf16)
    for j, c in steps:
        take_sibling(0, j, c)
    near = span(h * CORES * tile_rows, CORES * tile_rows)
    product[...] = jnp.dot(spread[:, near], coupling[near, :], preferred_element_type=f32)
    take_x(*steps[-1])
    for j in range(shells):
        group = lax.rem(s + j, shells)
        for d in range(1, chips):
            for c in range(pieces):
                take_sibling(d, j, c)
            first_row = lax.rem(h - d + chips, chips) * CORES * tile_rows + group * own
            spots = [span(first_row + i * tile_rows, own) for i in range(CORES)]
            product[...] += jnp.dot(
                jnp.concatenate([spread[:, at] for at in spots], axis=1),
                jnp.concatenate([coupling[at, :] for at in spots], axis=0),
                preferred_element_type=f32,
            )
    real, imag = combine(product[...])
    out_ref[0, 0, 0] = owned[:, :width] - real
    out_ref[1, 0, 0] = owned[:, width:] - imag

    for j, c in steps:
        group = lax.rem(s + j, shells)
        for o in range(1, shells):
            y_copy(o, j, c, group).wait_send()
        f_copy(0, j, c, group, r).wait_send()
        for d in range(1, chips):
            x_copy(d, j, c, group, r).wait_send()
            f_copy(d, j, c, group, lax.rem(h - d + chips, chips) * CORES + core).wait_send()

    @pl.when(col < cols - 1)
    def _():
        for i in range(passes):
            m_copy(i).wait_send()


def body(sizes, left_basis, right_basis, point_weight, shell_index, green_table, pivot_rows, diag_inverse):
    shells, rows, cols = sizes
    chips = rows // CORES
    tile_rows, points = left_basis.shape[1:]
    width = right_basis.shape[2]
    own = tile_rows // shells
    chunk = own // 4
    half = chunk
    pieces = own // chunk
    all_rows = rows * tile_rows
    bf16, f32 = jnp.bfloat16, jnp.float32
    vmem = pl.BlockSpec(memory_space=pltpu.VMEM)
    sems = pltpu.SemaphoreType.DMA
    buffers = [
        ((2, tile_rows, points), bf16),
        ((2, points, width), bf16),
        (diag_inverse.shape, bf16),
        (point_weight.shape, f32),
        (shell_index.shape, jnp.int32),
        (green_table.shape[::-1], f32),
        (pivot_rows.shape, jnp.int32),
        ((points, 256), f32),
        ((points, 2 * width), bf16),
        ((2 * own, 2 * width), f32),
        ((tile_rows, 2 * width), f32),
        ((tile_rows, 2 * width), bf16),
        ((max(shells - 1, 1), tile_rows, 2 * width), bf16),
        ((all_rows, 2 * width), bf16),
        ((own, 2 * width), f32),
        ((own // half, 2, half, width), bf16),
        ((all_rows, pivot_rows.shape[0]), bf16),
        ((2 * own, all_rows), bf16),
    ]
    held = sum(math.prod(shape) * jnp.dtype(kind).itemsize for shape, kind in buffers)
    return pl.pallas_call(
        functools.partial(kernel, shells, rows, cols, chunk),
        out_shape=pltpu.VMEM((2, 1, 1, own, width), f32),
        in_specs=[pl.BlockSpec(memory_space=pltpu.HBM)] * 7,
        out_specs=vmem,
        scratch_shapes=[pltpu.VMEM(shape, kind) for shape, kind in buffers] + [
            sems((points // 256 + 6,)),
            sems((max(shells - 1, 1), shells, pieces)),
            sems((max(shells - 1, 1), shells, pieces)),
            sems((max(chips - 1, 1), shells, pieces)),
            sems((max(chips - 1, 1), shells, pieces)),
            sems((chips, shells, pieces)),
            sems((chips, shells, pieces)),
            sems((own // half,)),
            sems((own // half,)),
        ],
        compiler_params=pltpu.CompilerParams(
            collective_id=0, has_side_effects=True, vmem_limit_bytes=56 * 2**20
        ),
        cost_estimate=pl.CostEstimate(
            flops=2 * tile_rows * 2 * points * 2 * width + 4 * own * all_rows * 2 * width,
            bytes_accessed=8 * 2**20,
            transcendentals=0,
        ),
    )(left_basis, right_basis, point_weight, shell_index, green_table.T, pivot_rows, diag_inverse)


def solution(mesh):
    sizes = tuple(mesh.shape[name] for name in ("shell", "row", "col"))
    return jax.shard_map(
        functools.partial(body, sizes),
        mesh=mesh,
        in_specs=(
            P(None, "row", "shell"),
            P(None, "shell", "col"),
            P("shell"),
            P("shell"),
            P(),
            P(),
            P(),
        ),
        out_specs=P(None, "row", "shell", None, "col"),
        check_vma=False,
    )
```

```python
import functools
import math
import jax
import jax.numpy as jnp
from jax import lax
from jax.experimental import pallas as pl
from jax.experimental.pallas import tpu as pltpu
from jax.sharding import PartitionSpec as P

MESH = pl.DeviceIdType.MESH
CORES = 2


def kernel(shells, rows, cols, chunk, left_hbm, right_hbm, point_hbm, shell_hbm, green_hbm, pivot_hbm,
           inverse_hbm, out_ref, left_ref, right_ref, inverse_ref, point_ref, shell_ref, green_ref, pivot_ref, weights, weighted, product, part,
           outgoing, incoming, coupling, owned, mult, select, spread, in_sem, y_send, y_recv, x_send,
           x_recv, f_send, f_recv, m_send, m_recv):
    s = lax.axis_index("shell")
    r = lax.axis_index("row")
    col = lax.axis_index("col")
    chips = rows // CORES
    h = r // CORES
    core = lax.rem(r, CORES)
    sibling = h * CORES + (CORES - 1 - core)
    points = right_ref.shape[1]
    width = right_ref.shape[2]
    tile_rows = left_ref.shape[1]
    own = tile_rows // shells
    pieces = own // chunk
    half = mult.shape[2]
    batch = 2 * chunk
    halves = batch // half
    bf16, f32 = jnp.bfloat16, jnp.float32

    slab = 256
    slabs = points // slab
    right_in = [
        pltpu.make_async_copy(
            right_hbm.at[:, pl.ds(b * slab, slab)], right_ref.at[:, pl.ds(b * slab, slab)], in_sem.at[b]
        )
        for b in range(slabs)
    ]
    left_in = pltpu.make_async_copy(left_hbm, left_ref, in_sem.at[slabs])
    inverse_in = pltpu.make_async_copy(inverse_hbm, inverse_ref, in_sem.at[slabs + 1])
    small_in = [
        pltpu.make_async_copy(source, target, in_sem.at[slabs + 2 + i])
        for i, (source, target) in enumerate([
            (point_hbm, point_ref), (shell_hbm, shell_ref), (green_hbm, green_ref), (pivot_hbm, pivot_ref)
        ])
    ]
    for copy in small_in[:3]:
        copy.start()
    right_in[0].start()
    left_in.start()
    for copy in right_in[1:]:
        copy.start()
    small_in[3].start()

    @pl.when(col == 0)
    def _():
        inverse_in.start()

    barrier = pltpu.get_barrier_semaphore()

    def greet(**where):
        pl.semaphore_signal(barrier, inc=1, device_id=where, device_id_type=MESH)

    for o in range(1, shells):
        greet(shell=lax.rem(s + o, shells))
    for d in range(1, chips):
        greet(row=lax.rem(h + d, chips) * CORES + core)
    greet(row=sibling)

    @pl.when(col > 0)
    def _():
        greet(col=col - 1)

    @pl.when(col < cols - 1)
    def _():
        greet(col=col + 1)

    for copy in small_in[:3]:
        copy.wait()
    count = green_ref.shape[1]
    padded = -(-count // 16) * 16
    index = shell_ref[...].reshape(1, points)
    match = lax.broadcasted_iota(jnp.int32, (padded, points), 0) == index

    def pieces_of(value):
        first = value.astype(bf16).astype(f32)
        second = (value - first).astype(bf16).astype(f32)
        return first, second, value - first - second

    hot = [jnp.where(match, piece, 0.0).astype(bf16) for piece in pieces_of(point_ref[...].reshape(1, points))]
    square = (padded, count)
    same = lax.broadcasted_iota(jnp.int32, square, 0) == lax.broadcasted_iota(jnp.int32, square, 1)
    table = jnp.concatenate(
        [
            jnp.broadcast_to(
                jnp.sum(
                    jnp.where(same, jnp.broadcast_to(green_ref[i : i + 1, :], square), 0.0),
                    axis=1, keepdims=True,
                ),
                (padded, 128),
            )
            for i in range(2)
        ],
        axis=1,
    )
    green = [piece.astype(bf16) for piece in pieces_of(table)]
    pairs = [(i, j) for i in range(3) for j in range(3 - i)]
    weights[...] = lax.dot_general(
        jnp.concatenate([hot[i] for i, _ in pairs], axis=0),
        jnp.concatenate([green[j] for _, j in pairs], axis=0),
        (((0,), (0,)), ((), ())),
        preferred_element_type=f32,
    )

    def span(first, size):
        return pl.ds(pl.multiple_of(first, size), size)

    def y_copy(o, j, c, group):
        at = span(group * own + c * chunk, chunk)
        return pltpu.make_async_remote_copy(
            src_ref=outgoing.at[at], dst_ref=incoming.at[o - 1, at],
            send_sem=y_send.at[o - 1, j, c], recv_sem=y_recv.at[o - 1, j, c],
            device_id={"shell": lax.rem(s + o, shells)}, device_id_type=MESH,
        )

    def x_copy(d, j, c, group, row):
        at = span(row * tile_rows + group * own + c * chunk, chunk)
        return pltpu.make_async_remote_copy(
            src_ref=coupling.at[at], dst_ref=coupling.at[at],
            send_sem=x_send.at[d - 1, j, c], recv_sem=x_recv.at[d - 1, j, c],
            device_id={"row": lax.rem(h + d, chips) * CORES + core}, device_id_type=MESH,
        )

    def f_copy(d, j, c, group, row):
        at = span(row * tile_rows + group * own + c * chunk, chunk)
        return pltpu.make_async_remote_copy(
            src_ref=coupling.at[at], dst_ref=coupling.at[at],
            send_sem=f_send.at[d, j, c], recv_sem=f_recv.at[d, j, c],
            device_id={"row": sibling}, device_id_type=MESH,
        )

    def m_copy(i):
        return pltpu.make_async_remote_copy(
            src_ref=mult.at[i], dst_ref=mult.at[i], send_sem=m_send.at[i], recv_sem=m_recv.at[i],
            device_id={"col": col + 1}, device_id_type=MESH,
        )

    def left_rows(group, at):
        rows_at = span(group * own, own)
        return jnp.concatenate([left_ref[0, rows_at, at], left_ref[1, rows_at, at]], axis=0)

    def combine(first_row, size):
        top = product[first_row : first_row + size, :]
        low = product[own + first_row : own + first_row + size, :]
        return top[:, :width] - low[:, width:], top[:, width:] + low[:, :width]

    first = lax.rem(s + 1, shells)
    for b in range(slabs):
        at = pl.ds(b * slab, slab)
        right_in[b].wait()
        w_real = jnp.concatenate([weights[at, :128]] * (width // 128), axis=1)
        w_imag = jnp.concatenate([weights[at, 128:]] * (width // 128), axis=1)
        b_real = right_ref[0, at, :].astype(f32)
        b_imag = right_ref[1, at, :].astype(f32)
        weighted[at, :width] = (w_real * b_real - w_imag * b_imag).astype(bf16)
        weighted[at, width:] = (w_real * b_imag + w_imag * b_real).astype(bf16)
        if b == 0:
            left_in.wait()
        term = jnp.dot(left_rows(first, at), weighted[at, :], preferred_element_type=f32)
        product[...] = term if b == 0 else product[...] + term

    for k in range(shells):
        group = lax.rem(s + 1 + k, shells)
        if k > 0:
            product[...] = jnp.dot(
                left_rows(group, pl.ds(0, points)), weighted[...], preferred_element_type=f32
            )
        if k == 0:
            line = jnp.minimum(col, 1) + jnp.minimum(cols - 1 - col, 1)
            pl.semaphore_wait(barrier, shells - 1 + chips + line)
        for c in range(pieces):
            at = span(group * own + c * chunk, chunk)
            real, imag = combine(c * chunk, chunk)
            part[at, :width] = real
            part[at, width:] = imag
            outgoing[at, :width] = real.astype(bf16)
            outgoing[at, width:] = imag.astype(bf16)
            for o in range(1, shells):
                y_copy(o, (1 + k - o) % shells, c, group).start()

    def choose(i):
        pivots = pivot_ref[...].reshape(1, -1)
        line = lax.broadcasted_iota(jnp.int32, (128, pivots.shape[1]), 0) + i * 128
        select[i * 128 : (i + 1) * 128, :] = jnp.where(line == pivots, 1.0, 0.0).astype(bf16)

    def take_y(j, c):
        group = lax.rem(s + j, shells)
        at = span(group * own + c * chunk, chunk)
        total = part[at, :]
        for o in range(1, shells):
            y_copy(o, j, c, group).wait_recv()
            total = total + incoming[o - 1, at, :].astype(f32)
        coupling[span(r * tile_rows + group * own + c * chunk, chunk), :] = total.astype(bf16)
        if j == 0:
            owned[c * chunk : (c + 1) * chunk, :] = total
        for d in range(1, chips):
            x_copy(d, j, c, group, r).start()
        f_copy(0, j, c, group, r).start()
        if j == 0 and (c + 1) * chunk % batch == 0:

            @pl.when(col == 0)
            def _():
                base = (c + 1) * chunk - batch
                if base == 0:
                    inverse_in.wait()
                panel = owned[base : base + batch, :]
                high = panel.astype(bf16)
                low = (panel - high.astype(f32)).astype(bf16)
                four = jnp.concatenate(
                    [high[:, :width], low[:, :width], high[:, width:], low[:, width:]], axis=0
                )
                by_real = jnp.dot(four, inverse_ref[0], preferred_element_type=f32)
                by_imag = jnp.dot(four, inverse_ref[1], preferred_element_type=f32)

                def pick(value, at):
                    return value[at : at + batch] + value[at + batch : at + 2 * batch]

                m_real = (pick(by_real, 0) - pick(by_imag, 2 * batch)).astype(bf16)
                m_imag = (pick(by_imag, 0) + pick(by_real, 2 * batch)).astype(bf16)
                for p in range(halves):
                    i = base // half + p
                    mult[i, 0] = m_real[p * half : (p + 1) * half]
                    mult[i, 1] = m_imag[p * half : (p + 1) * half]
                    if cols > 1:
                        m_copy(i).start()

    def take_x(j, c):
        group = lax.rem(s + j, shells)
        for d in range(1, chips):
            row = lax.rem(h - d + chips, chips) * CORES + core
            x_copy(d, j, c, group, row).wait_recv()
            f_copy(d, j, c, group, row).start()

    passes = own // half

    def pass_mult(turn):
        for i in range(passes):
            k, odd = divmod(turn - i, 2)
            if odd == 0 and 0 < k < cols - 1:

                @pl.when(col == k)
                def _():
                    m_copy(i).wait_recv()
                    m_copy(i).start()

    def take_sibling(d, j, c):
        group = lax.rem(s + j, shells)
        row = lax.rem(h - d + chips, chips) * CORES + (CORES - 1 - core)
        f_copy(d, j, c, group, row).wait_recv()

    steps = [(j, c) for j in range(shells) for c in range(pieces)]
    lag = 3
    slices = select.shape[0] // 128
    small_in[3].wait()
    for n, (j, c) in enumerate(steps):
        take_y(j, c)
        pass_mult(n - 1)
        if n >= lag:
            take_x(*steps[n - lag])
        for i in range(n * slices // len(steps), (n + 1) * slices // len(steps)):
            choose(i)

    for turn in range(len(steps) - 1, passes + 2 * cols):
        pass_mult(turn)

    @pl.when((col == cols - 1) & (col > 0))
    def _():
        for i in range(passes):
            m_copy(i).wait_recv()

    factors = jnp.concatenate([mult[i, p] for p in range(2) for i in range(passes)], axis=0)
    spread[...] = lax.dot_general(
        factors, select[...], (((1,), (1,)), ((), ())), preferred_element_type=f32
    ).astype(bf16)
    for j, c in steps:
        take_sibling(0, j, c)
    near = span(h * CORES * tile_rows, CORES * tile_rows)
    product[...] = jnp.dot(spread[:, near], coupling[near, :], preferred_element_type=f32)
    for j in range(shells):
        if j == shells - 1:
            for step in steps[-lag:]:
                take_x(*step)
        group = lax.rem(s + j, shells)
        for d in range(1, chips):
            for c in range(pieces):
                take_sibling(d, j, c)
            first_row = lax.rem(h - d + chips, chips) * CORES * tile_rows + group * own
            spots = [span(first_row + i * tile_rows, own) for i in range(CORES)]
            product[...] += jnp.dot(
                jnp.concatenate([spread[:, at] for at in spots], axis=1),
                jnp.concatenate([coupling[at, :] for at in spots], axis=0),
                preferred_element_type=f32,
            )
    real, imag = combine(0, own)
    out_ref[0, 0, 0] = owned[:, :width] - real
    out_ref[1, 0, 0] = owned[:, width:] - imag

    for j, c in steps:
        group = lax.rem(s + j, shells)
        for o in range(1, shells):
            y_copy(o, j, c, group).wait_send()
        f_copy(0, j, c, group, r).wait_send()
        for d in range(1, chips):
            x_copy(d, j, c, group, r).wait_send()
            f_copy(d, j, c, group, lax.rem(h - d + chips, chips) * CORES + core).wait_send()

    @pl.when(col < cols - 1)
    def _():
        for i in range(passes):
            m_copy(i).wait_send()


def body(sizes, left_basis, right_basis, point_weight, shell_index, green_table, pivot_rows, diag_inverse):
    shells, rows, cols = sizes
    chips = rows // CORES
    tile_rows, points = left_basis.shape[1:]
    width = right_basis.shape[2]
    own = tile_rows // shells
    chunk = own // 8
    half = chunk
    pieces = own // chunk
    all_rows = rows * tile_rows
    bf16, f32 = jnp.bfloat16, jnp.float32
    vmem = pl.BlockSpec(memory_space=pltpu.VMEM)
    sems = pltpu.SemaphoreType.DMA
    buffers = [
        ((2, tile_rows, points), bf16),
        ((2, points, width), bf16),
        (diag_inverse.shape, bf16),
        (point_weight.shape, f32),
        (shell_index.shape, jnp.int32),
        (green_table.shape[::-1], f32),
        (pivot_rows.shape, jnp.int32),
        ((points, 256), f32),
        ((points, 2 * width), bf16),
        ((2 * own, 2 * width), f32),
        ((tile_rows, 2 * width), f32),
        ((tile_rows, 2 * width), bf16),
        ((max(shells - 1, 1), tile_rows, 2 * width), bf16),
        ((all_rows, 2 * width), bf16),
        ((own, 2 * width), f32),
        ((own // half, 2, half, width), bf16),
        ((all_rows, pivot_rows.shape[0]), bf16),
        ((2 * own, all_rows), bf16),
    ]
    held = sum(math.prod(shape) * jnp.dtype(kind).itemsize for shape, kind in buffers)
    return pl.pallas_call(
        functools.partial(kernel, shells, rows, cols, chunk),
        out_shape=pltpu.VMEM((2, 1, 1, own, width), f32),
        in_specs=[pl.BlockSpec(memory_space=pltpu.HBM)] * 7,
        out_specs=vmem,
        scratch_shapes=[pltpu.VMEM(shape, kind) for shape, kind in buffers] + [
            sems((points // 256 + 6,)),
            sems((max(shells - 1, 1), shells, pieces)),
            sems((max(shells - 1, 1), shells, pieces)),
            sems((max(chips - 1, 1), shells, pieces)),
            sems((max(chips - 1, 1), shells, pieces)),
            sems((chips, shells, pieces)),
            sems((chips, shells, pieces)),
            sems((own // half,)),
            sems((own // half,)),
        ],
        compiler_params=pltpu.CompilerParams(
            collective_id=0, has_side_effects=True, vmem_limit_bytes=56 * 2**20
        ),
        cost_estimate=pl.CostEstimate(
            flops=2 * tile_rows * 2 * points * 2 * width + 4 * own * all_rows * 2 * width,
            bytes_accessed=8 * 2**20,
            transcendentals=0,
        ),
    )(left_basis, right_basis, point_weight, shell_index, green_table.T, pivot_rows, diag_inverse)


def solution(mesh):
    sizes = tuple(mesh.shape[name] for name in ("shell", "row", "col"))
    return jax.shard_map(
        functools.partial(body, sizes),
        mesh=mesh,
        in_specs=(
            P(None, "row", "shell"),
            P(None, "shell", "col"),
            P("shell"),
            P("shell"),
            P(),
            P(),
            P(),
        ),
        out_specs=P(None, "row", "shell", None, "col"),
        check_vma=False,
    )
```

```python
import functools
import math
import jax
import jax.numpy as jnp
from jax import lax
from jax.experimental import pallas as pl
from jax.experimental.pallas import tpu as pltpu
from jax.sharding import PartitionSpec as P

MESH = pl.DeviceIdType.MESH
CORES = 2


def kernel(shells, rows, cols, chunk, left_hbm, right_hbm, point_hbm, shell_hbm, green_hbm, pivot_hbm,
           inverse_hbm, out_ref, left_ref, right_ref, inverse_ref, point_ref, shell_ref, green_ref, pivot_ref, weights, weighted, product, part,
           outgoing, incoming, coupling, owned, mult, select, spread, in_sem, y_send, y_recv, x_send,
           x_recv, f_send, f_recv, m_send, m_recv):
    s = lax.axis_index("shell")
    r = lax.axis_index("row")
    col = lax.axis_index("col")
    chips = rows // CORES
    h = r // CORES
    core = lax.rem(r, CORES)
    sibling = h * CORES + (CORES - 1 - core)
    points = right_ref.shape[1]
    width = right_ref.shape[2]
    tile_rows = left_ref.shape[1]
    own = tile_rows // shells
    pieces = own // chunk
    half = mult.shape[2]
    batch = chunk
    halves = batch // half
    bf16, f32 = jnp.bfloat16, jnp.float32

    slab = 256
    slabs = points // slab
    right_in = [
        pltpu.make_async_copy(
            right_hbm.at[:, pl.ds(b * slab, slab)], right_ref.at[:, pl.ds(b * slab, slab)], in_sem.at[b]
        )
        for b in range(slabs)
    ]
    left_in = pltpu.make_async_copy(left_hbm, left_ref, in_sem.at[slabs])
    inverse_in = pltpu.make_async_copy(inverse_hbm, inverse_ref, in_sem.at[slabs + 1])
    small_in = [
        pltpu.make_async_copy(source, target, in_sem.at[slabs + 2 + i])
        for i, (source, target) in enumerate([
            (point_hbm, point_ref), (shell_hbm, shell_ref), (green_hbm, green_ref), (pivot_hbm, pivot_ref)
        ])
    ]
    for copy in small_in[:3]:
        copy.start()
    right_in[0].start()
    left_in.start()
    for copy in right_in[1:]:
        copy.start()
    small_in[3].start()

    @pl.when(col == 0)
    def _():
        inverse_in.start()

    barrier = pltpu.get_barrier_semaphore()

    def greet(**where):
        pl.semaphore_signal(barrier, inc=1, device_id=where, device_id_type=MESH)

    for o in range(1, shells):
        greet(shell=lax.rem(s + o, shells))
    for d in range(1, chips):
        greet(row=lax.rem(h + d, chips) * CORES + core)
    greet(row=sibling)

    @pl.when(col > 0)
    def _():
        greet(col=col - 1)

    @pl.when(col < cols - 1)
    def _():
        greet(col=col + 1)

    for copy in small_in[:3]:
        copy.wait()
    count = green_ref.shape[1]
    padded = -(-count // 16) * 16
    index = shell_ref[...].reshape(1, points)
    match = lax.broadcasted_iota(jnp.int32, (padded, points), 0) == index

    def pieces_of(value):
        first = value.astype(bf16).astype(f32)
        second = (value - first).astype(bf16).astype(f32)
        return first, second, value - first - second

    hot = [jnp.where(match, piece, 0.0).astype(bf16) for piece in pieces_of(point_ref[...].reshape(1, points))]
    square = (padded, count)
    same = lax.broadcasted_iota(jnp.int32, square, 0) == lax.broadcasted_iota(jnp.int32, square, 1)
    table = jnp.concatenate(
        [
            jnp.broadcast_to(
                jnp.sum(
                    jnp.where(same, jnp.broadcast_to(green_ref[i : i + 1, :], square), 0.0),
                    axis=1, keepdims=True,
                ),
                (padded, 128),
            )
            for i in range(2)
        ],
        axis=1,
    )
    green = [piece.astype(bf16) for piece in pieces_of(table)]
    pairs = [(i, j) for i in range(3) for j in range(3 - i)]
    weights[...] = lax.dot_general(
        jnp.concatenate([hot[i] for i, _ in pairs], axis=0),
        jnp.concatenate([green[j] for _, j in pairs], axis=0),
        (((0,), (0,)), ((), ())),
        preferred_element_type=f32,
    )

    def span(first, size):
        return pl.ds(pl.multiple_of(first, size), size)

    def y_copy(o, j, c, group):
        at = span(group * own + c * chunk, chunk)
        return pltpu.make_async_remote_copy(
            src_ref=outgoing.at[at], dst_ref=incoming.at[o - 1, at],
            send_sem=y_send.at[o - 1, j, c], recv_sem=y_recv.at[o - 1, j, c],
            device_id={"shell": lax.rem(s + o, shells)}, device_id_type=MESH,
        )

    def x_copy(d, j, c, group, row):
        at = span(row * tile_rows + group * own + c * chunk, chunk)
        return pltpu.make_async_remote_copy(
            src_ref=coupling.at[at], dst_ref=coupling.at[at],
            send_sem=x_send.at[d - 1, j, c], recv_sem=x_recv.at[d - 1, j, c],
            device_id={"row": lax.rem(h + d, chips) * CORES + core}, device_id_type=MESH,
        )

    def f_copy(d, j, c, group, row):
        at = span(row * tile_rows + group * own + c * chunk, chunk)
        return pltpu.make_async_remote_copy(
            src_ref=coupling.at[at], dst_ref=coupling.at[at],
            send_sem=f_send.at[d, j, c], recv_sem=f_recv.at[d, j, c],
            device_id={"row": sibling}, device_id_type=MESH,
        )

    def m_copy(i):
        return pltpu.make_async_remote_copy(
            src_ref=mult.at[i], dst_ref=mult.at[i], send_sem=m_send.at[i], recv_sem=m_recv.at[i],
            device_id={"col": col + 1}, device_id_type=MESH,
        )

    def left_rows(group, at):
        rows_at = span(group * own, own)
        return jnp.concatenate([left_ref[0, rows_at, at], left_ref[1, rows_at, at]], axis=0)

    def combine(first_row, size):
        top = product[first_row : first_row + size, :]
        low = product[own + first_row : own + first_row + size, :]
        return top[:, :width] - low[:, width:], top[:, width:] + low[:, :width]

    first = lax.rem(s + 1, shells)
    for b in range(slabs):
        at = pl.ds(b * slab, slab)
        right_in[b].wait()
        w_real = jnp.concatenate([weights[at, :128]] * (width // 128), axis=1)
        w_imag = jnp.concatenate([weights[at, 128:]] * (width // 128), axis=1)
        b_real = right_ref[0, at, :].astype(f32)
        b_imag = right_ref[1, at, :].astype(f32)
        weighted[at, :width] = (w_real * b_real - w_imag * b_imag).astype(bf16)
        weighted[at, width:] = (w_real * b_imag + w_imag * b_real).astype(bf16)
        if b == 0:
            left_in.wait()
        term = jnp.dot(left_rows(first, at), weighted[at, :], preferred_element_type=f32)
        product[...] = term if b == 0 else product[...] + term

    for k in range(shells):
        group = lax.rem(s + 1 + k, shells)
        if k > 0:
            product[...] = jnp.dot(
                left_rows(group, pl.ds(0, points)), weighted[...], preferred_element_type=f32
            )
        if k == 0:
            line = jnp.minimum(col, 1) + jnp.minimum(cols - 1 - col, 1)
            pl.semaphore_wait(barrier, shells - 1 + chips + line)
        for c in range(pieces):
            at = span(group * own + c * chunk, chunk)
            real, imag = combine(c * chunk, chunk)
            part[at, :width] = real
            part[at, width:] = imag
            outgoing[at, :width] = real.astype(bf16)
            outgoing[at, width:] = imag.astype(bf16)
            for o in range(1, shells):
                y_copy(o, (1 + k - o) % shells, c, group).start()

    def choose(i):
        pivots = pivot_ref[...].reshape(1, -1)
        line = lax.broadcasted_iota(jnp.int32, (128, pivots.shape[1]), 0) + i * 128
        select[i * 128 : (i + 1) * 128, :] = jnp.where(line == pivots, 1.0, 0.0).astype(bf16)

    def take_y(j, c):
        group = lax.rem(s + j, shells)
        at = span(group * own + c * chunk, chunk)
        total = part[at, :]
        for o in range(1, shells):
            y_copy(o, j, c, group).wait_recv()
            total = total + incoming[o - 1, at, :].astype(f32)
        coupling[span(r * tile_rows + group * own + c * chunk, chunk), :] = total.astype(bf16)
        if j == 0:
            owned[c * chunk : (c + 1) * chunk, :] = total
        for d in range(1, chips):
            x_copy(d, j, c, group, r).start()
        f_copy(0, j, c, group, r).start()
        if j == 0 and (c + 1) * chunk % batch == 0:

            @pl.when(col == 0)
            def _():
                base = (c + 1) * chunk - batch
                if base == 0:
                    inverse_in.wait()
                panel = owned[base : base + batch, :]
                high = panel.astype(bf16)
                low = (panel - high.astype(f32)).astype(bf16)
                four = jnp.concatenate(
                    [high[:, :width], low[:, :width], high[:, width:], low[:, width:]], axis=0
                )
                by_real = jnp.dot(four, inverse_ref[0], preferred_element_type=f32)
                by_imag = jnp.dot(four, inverse_ref[1], preferred_element_type=f32)

                def pick(value, at):
                    return value[at : at + batch] + value[at + batch : at + 2 * batch]

                m_real = (pick(by_real, 0) - pick(by_imag, 2 * batch)).astype(bf16)
                m_imag = (pick(by_imag, 0) + pick(by_real, 2 * batch)).astype(bf16)
                for p in range(halves):
                    i = base // half + p
                    mult[i, 0] = m_real[p * half : (p + 1) * half]
                    mult[i, 1] = m_imag[p * half : (p + 1) * half]
                    if cols > 1:
                        m_copy(i).start()

    def take_x(j, c):
        group = lax.rem(s + j, shells)
        for d in range(1, chips):
            row = lax.rem(h - d + chips, chips) * CORES + core
            x_copy(d, j, c, group, row).wait_recv()
            f_copy(d, j, c, group, row).start()

    passes = own // half

    def pass_mult(turn):
        for i in range(passes):
            k, odd = divmod(turn - i, 2)
            if odd == 0 and 0 < k < cols - 1:

                @pl.when(col == k)
                def _():
                    m_copy(i).wait_recv()
                    m_copy(i).start()

    def take_sibling(d, j, c):
        group = lax.rem(s + j, shells)
        row = lax.rem(h - d + chips, chips) * CORES + (CORES - 1 - core)
        f_copy(d, j, c, group, row).wait_recv()

    steps = [(j, c) for j in range(shells) for c in range(pieces)]
    lag = 2
    slices = select.shape[0] // 128
    small_in[3].wait()
    for n, (j, c) in enumerate(steps):
        take_y(j, c)
        pass_mult(n)
        if n >= lag:
            take_x(*steps[n - lag])
        for i in range(n * slices // len(steps), (n + 1) * slices // len(steps)):
            choose(i)

    for turn in range(len(steps), passes + 2 * cols):
        pass_mult(turn)

    @pl.when((col == cols - 1) & (col > 0))
    def _():
        for i in range(passes):
            m_copy(i).wait_recv()

    factors = jnp.concatenate([mult[i, p] for p in range(2) for i in range(passes)], axis=0)
    spread[...] = lax.dot_general(
        factors, select[...], (((1,), (1,)), ((), ())), preferred_element_type=f32
    ).astype(bf16)
    for j, c in steps:
        take_sibling(0, j, c)
    near = span(h * CORES * tile_rows, CORES * tile_rows)
    product[...] = jnp.dot(spread[:, near], coupling[near, :], preferred_element_type=f32)
    for j in range(shells):
        if j == shells - 1:
            for step in steps[-lag:]:
                take_x(*step)
        group = lax.rem(s + j, shells)
        for d in range(1, chips):
            for c in range(pieces):
                take_sibling(d, j, c)
            first_row = lax.rem(h - d + chips, chips) * CORES * tile_rows + group * own
            spots = [span(first_row + i * tile_rows, own) for i in range(CORES)]
            product[...] += jnp.dot(
                jnp.concatenate([spread[:, at] for at in spots], axis=1),
                jnp.concatenate([coupling[at, :] for at in spots], axis=0),
                preferred_element_type=f32,
            )
    real, imag = combine(0, own)
    out_ref[0, 0, 0] = owned[:, :width] - real
    out_ref[1, 0, 0] = owned[:, width:] - imag

    for j, c in steps:
        group = lax.rem(s + j, shells)
        for o in range(1, shells):
            y_copy(o, j, c, group).wait_send()
        f_copy(0, j, c, group, r).wait_send()
        for d in range(1, chips):
            x_copy(d, j, c, group, r).wait_send()
            f_copy(d, j, c, group, lax.rem(h - d + chips, chips) * CORES + core).wait_send()

    @pl.when(col < cols - 1)
    def _():
        for i in range(passes):
            m_copy(i).wait_send()


def body(sizes, left_basis, right_basis, point_weight, shell_index, green_table, pivot_rows, diag_inverse):
    shells, rows, cols = sizes
    chips = rows // CORES
    tile_rows, points = left_basis.shape[1:]
    width = right_basis.shape[2]
    own = tile_rows // shells
    chunk = own // 4
    half = chunk
    pieces = own // chunk
    all_rows = rows * tile_rows
    bf16, f32 = jnp.bfloat16, jnp.float32
    vmem = pl.BlockSpec(memory_space=pltpu.VMEM)
    sems = pltpu.SemaphoreType.DMA
    buffers = [
        ((2, tile_rows, points), bf16),
        ((2, points, width), bf16),
        (diag_inverse.shape, bf16),
        (point_weight.shape, f32),
        (shell_index.shape, jnp.int32),
        (green_table.shape[::-1], f32),
        (pivot_rows.shape, jnp.int32),
        ((points, 256), f32),
        ((points, 2 * width), bf16),
        ((2 * own, 2 * width), f32),
        ((tile_rows, 2 * width), f32),
        ((tile_rows, 2 * width), bf16),
        ((max(shells - 1, 1), tile_rows, 2 * width), bf16),
        ((all_rows, 2 * width), bf16),
        ((own, 2 * width), f32),
        ((own // half, 2, half, width), bf16),
        ((all_rows, pivot_rows.shape[0]), bf16),
        ((2 * own, all_rows), bf16),
    ]
    held = sum(math.prod(shape) * jnp.dtype(kind).itemsize for shape, kind in buffers)
    return pl.pallas_call(
        functools.partial(kernel, shells, rows, cols, chunk),
        out_shape=pltpu.VMEM((2, 1, 1, own, width), f32),
        in_specs=[pl.BlockSpec(memory_space=pltpu.HBM)] * 7,
        out_specs=vmem,
        scratch_shapes=[pltpu.VMEM(shape, kind) for shape, kind in buffers] + [
            sems((points // 256 + 6,)),
            sems((max(shells - 1, 1), shells, pieces)),
            sems((max(shells - 1, 1), shells, pieces)),
            sems((max(chips - 1, 1), shells, pieces)),
            sems((max(chips - 1, 1), shells, pieces)),
            sems((chips, shells, pieces)),
            sems((chips, shells, pieces)),
            sems((own // half,)),
            sems((own // half,)),
        ],
        compiler_params=pltpu.CompilerParams(
            collective_id=0, has_side_effects=True, vmem_limit_bytes=56 * 2**20
        ),
        cost_estimate=pl.CostEstimate(
            flops=2 * tile_rows * 2 * points * 2 * width + 4 * own * all_rows * 2 * width,
            bytes_accessed=8 * 2**20,
            transcendentals=0,
        ),
    )(left_basis, right_basis, point_weight, shell_index, green_table.T, pivot_rows, diag_inverse)


def solution(mesh):
    sizes = tuple(mesh.shape[name] for name in ("shell", "row", "col"))
    return jax.shard_map(
        functools.partial(body, sizes),
        mesh=mesh,
        in_specs=(
            P(None, "row", "shell"),
            P(None, "shell", "col"),
            P("shell"),
            P("shell"),
            P(),
            P(),
            P(),
        ),
        out_specs=P(None, "row", "shell", None, "col"),
        check_vma=False,
    )
```

```python
import functools
import math
import jax
import jax.numpy as jnp
from jax import lax
from jax.experimental import pallas as pl
from jax.experimental.pallas import tpu as pltpu
from jax.sharding import PartitionSpec as P

MESH = pl.DeviceIdType.MESH
CORES = 2


def kernel(shells, rows, cols, chunk, left_hbm, right_hbm, point_hbm, shell_hbm, green_hbm, pivot_hbm,
           inverse_hbm, out_ref, left_ref, right_ref, inverse_ref, point_ref, shell_ref, green_ref, pivot_ref, weights, weighted, product, part,
           outgoing, incoming, coupling, owned, mult, select, spread, in_sem, y_send, y_recv, x_send,
           x_recv, f_send, f_recv, m_send, m_recv):
    s = lax.axis_index("shell")
    r = lax.axis_index("row")
    col = lax.axis_index("col")
    chips = rows // CORES
    h = r // CORES
    core = lax.rem(r, CORES)
    sibling = h * CORES + (CORES - 1 - core)
    points = right_ref.shape[1]
    width = right_ref.shape[2]
    tile_rows = left_ref.shape[1]
    own = tile_rows // shells
    pieces = own // chunk
    half = mult.shape[2]
    batch = chunk
    lanes = 128
    halves = batch // half
    bf16, f32 = jnp.bfloat16, jnp.float32

    slab = 256
    slabs = points // slab
    right_in = [
        pltpu.make_async_copy(
            right_hbm.at[:, pl.ds(b * slab, slab)], right_ref.at[:, pl.ds(b * slab, slab)], in_sem.at[b]
        )
        for b in range(slabs)
    ]
    left_in = pltpu.make_async_copy(left_hbm, left_ref, in_sem.at[slabs])
    inverse_in = pltpu.make_async_copy(inverse_hbm, inverse_ref, in_sem.at[slabs + 1])
    small_in = [
        pltpu.make_async_copy(source, target, in_sem.at[slabs + 2 + i])
        for i, (source, target) in enumerate([
            (point_hbm, point_ref), (shell_hbm, shell_ref), (green_hbm, green_ref), (pivot_hbm, pivot_ref)
        ])
    ]
    for copy in small_in[:3]:
        copy.start()
    right_in[0].start()
    left_in.start()
    for copy in right_in[1:]:
        copy.start()
    small_in[3].start()

    @pl.when(col == 0)
    def _():
        inverse_in.start()

    barrier = pltpu.get_barrier_semaphore()

    def greet(**where):
        pl.semaphore_signal(barrier, inc=1, device_id=where, device_id_type=MESH)

    for o in range(1, shells):
        greet(shell=lax.rem(s + o, shells))
    for d in range(1, chips):
        greet(row=lax.rem(h + d, chips) * CORES + core)
    greet(row=sibling)

    @pl.when(col > 0)
    def _():
        greet(col=col - 1)

    @pl.when(col < cols - 1)
    def _():
        greet(col=col + 1)

    for copy in small_in[:3]:
        copy.wait()
    count = green_ref.shape[1]
    padded = -(-count // 16) * 16
    index = shell_ref[...].reshape(1, points)
    match = lax.broadcasted_iota(jnp.int32, (padded, points), 0) == index

    def pieces_of(value):
        first = value.astype(bf16).astype(f32)
        second = (value - first).astype(bf16).astype(f32)
        return first, second, value - first - second

    hot = [jnp.where(match, piece, 0.0).astype(bf16) for piece in pieces_of(point_ref[...].reshape(1, points))]
    square = (padded, count)
    same = lax.broadcasted_iota(jnp.int32, square, 0) == lax.broadcasted_iota(jnp.int32, square, 1)
    table = jnp.concatenate(
        [
            jnp.broadcast_to(
                jnp.sum(
                    jnp.where(same, jnp.broadcast_to(green_ref[i : i + 1, :], square), 0.0),
                    axis=1, keepdims=True,
                ),
                (padded, 128),
            )
            for i in range(2)
        ],
        axis=1,
    )
    green = [piece.astype(bf16) for piece in pieces_of(table)]
    pairs = [(i, j) for i in range(3) for j in range(3 - i)]
    weights[...] = lax.dot_general(
        jnp.concatenate([hot[i] for i, _ in pairs], axis=0),
        jnp.concatenate([green[j] for _, j in pairs], axis=0),
        (((0,), (0,)), ((), ())),
        preferred_element_type=f32,
    )

    def span(first, size):
        return pl.ds(pl.multiple_of(first, size), size)

    def y_copy(o, j, c, group):
        at = span(group * own + c * chunk, chunk)
        return pltpu.make_async_remote_copy(
            src_ref=outgoing.at[at], dst_ref=incoming.at[o - 1, at],
            send_sem=y_send.at[o - 1, j, c], recv_sem=y_recv.at[o - 1, j, c],
            device_id={"shell": lax.rem(s + o, shells)}, device_id_type=MESH,
        )

    def x_copy(d, j, c, group, row):
        at = span(row * tile_rows + group * own + c * chunk, chunk)
        return pltpu.make_async_remote_copy(
            src_ref=coupling.at[at], dst_ref=coupling.at[at],
            send_sem=x_send.at[d - 1, j, c], recv_sem=x_recv.at[d - 1, j, c],
            device_id={"row": lax.rem(h + d, chips) * CORES + core}, device_id_type=MESH,
        )

    def f_copy(d, j, c, group, row):
        at = span(row * tile_rows + group * own + c * chunk, chunk)
        return pltpu.make_async_remote_copy(
            src_ref=coupling.at[at], dst_ref=coupling.at[at],
            send_sem=f_send.at[d, j, c], recv_sem=f_recv.at[d, j, c],
            device_id={"row": sibling}, device_id_type=MESH,
        )

    def m_copy(i):
        return pltpu.make_async_remote_copy(
            src_ref=mult.at[i], dst_ref=mult.at[i], send_sem=m_send.at[i], recv_sem=m_recv.at[i],
            device_id={"col": col + 1}, device_id_type=MESH,
        )

    def left_rows(group, at):
        rows_at = span(group * own, own)
        return jnp.concatenate([left_ref[0, rows_at, at], left_ref[1, rows_at, at]], axis=0)

    def combine(first_row, size):
        top = product[first_row : first_row + size, :]
        low = product[own + first_row : own + first_row + size, :]
        return top[:, :width] - low[:, width:], top[:, width:] + low[:, :width]

    first = lax.rem(s + 1, shells)
    every = pl.ds(0, points)
    for copy in right_in:
        copy.wait()
    left_in.wait()

    def pair(b):
        return pl.ds(b * lanes, lanes), pl.ds(width + b * lanes, lanes)

    for b in range(width // lanes):
        re, im = pair(b)
        w_real = weights[:, :lanes]
        w_imag = weights[:, lanes:]
        b_real = right_ref[0, :, re].astype(f32)
        b_imag = right_ref[1, :, re].astype(f32)
        both = jnp.concatenate(
            [
                (w_real * b_real - w_imag * b_imag).astype(bf16),
                (w_real * b_imag + w_imag * b_real).astype(bf16),
            ],
            axis=1,
        )
        weighted[:, re] = both[:, :lanes]
        weighted[:, im] = both[:, lanes:]
        term = jnp.dot(left_rows(first, every), both, preferred_element_type=f32)
        product[:, re] = term[:, :lanes]
        product[:, im] = term[:, lanes:]

    for k in range(shells):
        group = lax.rem(s + 1 + k, shells)
        if k > 0:
            product[...] = jnp.dot(
                left_rows(group, every), weighted[...], preferred_element_type=f32
            )
        if k == 0:
            line = jnp.minimum(col, 1) + jnp.minimum(cols - 1 - col, 1)
            pl.semaphore_wait(barrier, shells - 1 + chips + line)
        for c in range(pieces):
            at = span(group * own + c * chunk, chunk)
            real, imag = combine(c * chunk, chunk)
            part[at, :width] = real
            part[at, width:] = imag
            outgoing[at, :width] = real.astype(bf16)
            outgoing[at, width:] = imag.astype(bf16)
            for o in range(1, shells):
                y_copy(o, (1 + k - o) % shells, c, group).start()

    def choose(i):
        pivots = pivot_ref[...].reshape(1, -1)
        line = lax.broadcasted_iota(jnp.int32, (128, pivots.shape[1]), 0) + i * 128
        select[i * 128 : (i + 1) * 128, :] = jnp.where(line == pivots, 1.0, 0.0).astype(bf16)

    def take_y(j, c):
        group = lax.rem(s + j, shells)
        at = span(group * own + c * chunk, chunk)
        total = part[at, :]
        for o in range(1, shells):
            y_copy(o, j, c, group).wait_recv()
            total = total + incoming[o - 1, at, :].astype(f32)
        coupling[span(r * tile_rows + group * own + c * chunk, chunk), :] = total.astype(bf16)
        if j == 0:
            owned[c * chunk : (c + 1) * chunk, :] = total
        for d in range(1, chips):
            x_copy(d, j, c, group, r).start()
        f_copy(0, j, c, group, r).start()
        if j == 0 and (c + 1) * chunk % batch == 0:

            @pl.when(col == 0)
            def _():
                base = (c + 1) * chunk - batch
                if base == 0:
                    inverse_in.wait()
                panel = owned[base : base + batch, :]
                high = panel.astype(bf16)
                low = (panel - high.astype(f32)).astype(bf16)
                four = jnp.concatenate(
                    [high[:, :width], low[:, :width], high[:, width:], low[:, width:]], axis=0
                )
                by_real = jnp.dot(four, inverse_ref[0], preferred_element_type=f32)
                by_imag = jnp.dot(four, inverse_ref[1], preferred_element_type=f32)

                def pick(value, at):
                    return value[at : at + batch] + value[at + batch : at + 2 * batch]

                m_real = (pick(by_real, 0) - pick(by_imag, 2 * batch)).astype(bf16)
                m_imag = (pick(by_imag, 0) + pick(by_real, 2 * batch)).astype(bf16)
                for p in range(halves):
                    i = base // half + p
                    mult[i, 0] = m_real[p * half : (p + 1) * half]
                    mult[i, 1] = m_imag[p * half : (p + 1) * half]
                    if cols > 1:
                        m_copy(i).start()

    def take_x(j, c):
        group = lax.rem(s + j, shells)
        for d in range(1, chips):
            row = lax.rem(h - d + chips, chips) * CORES + core
            x_copy(d, j, c, group, row).wait_recv()
            f_copy(d, j, c, group, row).start()

    passes = own // half

    def pass_mult(turn):
        for i in range(passes):
            k, odd = divmod(turn - i, 2)
            if odd == 0 and 0 < k < cols - 1:

                @pl.when(col == k)
                def _():
                    m_copy(i).wait_recv()
                    m_copy(i).start()

    def take_sibling(d, j, c):
        group = lax.rem(s + j, shells)
        row = lax.rem(h - d + chips, chips) * CORES + (CORES - 1 - core)
        f_copy(d, j, c, group, row).wait_recv()

    steps = [(j, c) for j in range(shells) for c in range(pieces)]
    lag = 2
    slices = select.shape[0] // 128
    small_in[3].wait()
    for n, (j, c) in enumerate(steps):
        take_y(j, c)
        pass_mult(n)
        if n >= lag:
            take_x(*steps[n - lag])
        for i in range(n * slices // len(steps), (n + 1) * slices // len(steps)):
            choose(i)

    for turn in range(len(steps), passes + 2 * cols):
        pass_mult(turn)

    for step in steps[-lag:-1]:
        take_x(*step)

    @pl.when((col == cols - 1) & (col > 0))
    def _():
        for i in range(passes):
            m_copy(i).wait_recv()

    factors = jnp.concatenate([mult[i, p] for p in range(2) for i in range(passes)], axis=0)
    spread[...] = lax.dot_general(
        factors, select[...], (((1,), (1,)), ((), ())), preferred_element_type=f32
    ).astype(bf16)
    for j, c in steps:
        take_sibling(0, j, c)
    near = span(h * CORES * tile_rows, CORES * tile_rows)
    product[...] = jnp.dot(spread[:, near], coupling[near, :], preferred_element_type=f32)
    take_x(*steps[-1])

    def far_spots(j, d):
        group = lax.rem(s + j, shells)
        for c in range(pieces):
            take_sibling(d, j, c)
        first_row = lax.rem(h - d + chips, chips) * CORES * tile_rows + group * own
        return [span(first_row + i * tile_rows, own) for i in range(CORES)]

    def far_product(spots, re, im):
        return jnp.dot(
            jnp.concatenate([spread[:, at] for at in spots], axis=1),
            jnp.concatenate(
                [jnp.concatenate([coupling[at, re], coupling[at, im]], axis=1) for at in spots], axis=0
            ),
            preferred_element_type=f32,
        )

    for j in range(shells - 1):
        for d in range(1, chips):
            spots = far_spots(j, d)
            product[...] += far_product(spots, pl.ds(0, width), pl.ds(width, width))
    last = [at for d in range(1, chips) for at in far_spots(shells - 1, d)]
    for b in range(width // lanes):
        re, im = pair(b)
        four = jnp.concatenate([product[:, re], product[:, im]], axis=1) + far_product(last, re, im)
        out_ref[0, 0, 0, :, re] = owned[:, re] - (four[:own, :lanes] - four[own:, lanes:])
        out_ref[1, 0, 0, :, re] = owned[:, im] - (four[:own, lanes:] + four[own:, :lanes])

    for j, c in steps:
        group = lax.rem(s + j, shells)
        for o in range(1, shells):
            y_copy(o, j, c, group).wait_send()
        f_copy(0, j, c, group, r).wait_send()
        for d in range(1, chips):
            x_copy(d, j, c, group, r).wait_send()
            f_copy(d, j, c, group, lax.rem(h - d + chips, chips) * CORES + core).wait_send()

    @pl.when(col < cols - 1)
    def _():
        for i in range(passes):
            m_copy(i).wait_send()


def body(sizes, left_basis, right_basis, point_weight, shell_index, green_table, pivot_rows, diag_inverse):
    shells, rows, cols = sizes
    chips = rows // CORES
    tile_rows, points = left_basis.shape[1:]
    width = right_basis.shape[2]
    own = tile_rows // shells
    chunk = own // 4
    half = chunk
    pieces = own // chunk
    all_rows = rows * tile_rows
    bf16, f32 = jnp.bfloat16, jnp.float32
    vmem = pl.BlockSpec(memory_space=pltpu.VMEM)
    sems = pltpu.SemaphoreType.DMA
    buffers = [
        ((2, tile_rows, points), bf16),
        ((2, points, width), bf16),
        (diag_inverse.shape, bf16),
        (point_weight.shape, f32),
        (shell_index.shape, jnp.int32),
        (green_table.shape[::-1], f32),
        (pivot_rows.shape, jnp.int32),
        ((points, 256), f32),
        ((points, 2 * width), bf16),
        ((2 * own, 2 * width), f32),
        ((tile_rows, 2 * width), f32),
        ((tile_rows, 2 * width), bf16),
        ((max(shells - 1, 1), tile_rows, 2 * width), bf16),
        ((all_rows, 2 * width), bf16),
        ((own, 2 * width), f32),
        ((own // half, 2, half, width), bf16),
        ((all_rows, pivot_rows.shape[0]), bf16),
        ((2 * own, all_rows), bf16),
    ]
    held = sum(math.prod(shape) * jnp.dtype(kind).itemsize for shape, kind in buffers)
    return pl.pallas_call(
        functools.partial(kernel, shells, rows, cols, chunk),
        out_shape=pltpu.VMEM((2, 1, 1, own, width), f32),
        in_specs=[pl.BlockSpec(memory_space=pltpu.HBM)] * 7,
        out_specs=vmem,
        scratch_shapes=[pltpu.VMEM(shape, kind) for shape, kind in buffers] + [
            sems((points // 256 + 6,)),
            sems((max(shells - 1, 1), shells, pieces)),
            sems((max(shells - 1, 1), shells, pieces)),
            sems((max(chips - 1, 1), shells, pieces)),
            sems((max(chips - 1, 1), shells, pieces)),
            sems((chips, shells, pieces)),
            sems((chips, shells, pieces)),
            sems((own // half,)),
            sems((own // half,)),
        ],
        compiler_params=pltpu.CompilerParams(
            collective_id=0, has_side_effects=True, vmem_limit_bytes=56 * 2**20
        ),
        cost_estimate=pl.CostEstimate(
            flops=2 * tile_rows * 2 * points * 2 * width + 4 * own * all_rows * 2 * width,
            bytes_accessed=8 * 2**20,
            transcendentals=0,
        ),
    )(left_basis, right_basis, point_weight, shell_index, green_table.T, pivot_rows, diag_inverse)


def solution(mesh):
    sizes = tuple(mesh.shape[name] for name in ("shell", "row", "col"))
    return jax.shard_map(
        functools.partial(body, sizes),
        mesh=mesh,
        in_specs=(
            P(None, "row", "shell"),
            P(None, "shell", "col"),
            P("shell"),
            P("shell"),
            P(),
            P(),
            P(),
        ),
        out_specs=P(None, "row", "shell", None, "col"),
        check_vma=False,
    )
```

```python
import functools
import math
import jax
import jax.numpy as jnp
from jax import lax
from jax.experimental import pallas as pl
from jax.experimental.pallas import tpu as pltpu
from jax.sharding import PartitionSpec as P

MESH = pl.DeviceIdType.MESH
CORES = 2


def kernel(shells, rows, cols, chunk, left_hbm, right_hbm, point_hbm, shell_hbm, green_hbm, pivot_hbm,
           inverse_hbm, out_ref, left_ref, right_ref, inverse_ref, point_ref, shell_ref, green_ref, pivot_ref, weights, weighted, product, part,
           outgoing, incoming, coupling, owned, mult, select, spread, in_sem, y_send, y_recv, x_send,
           x_recv, f_send, f_recv, m_send, m_recv):
    s = lax.axis_index("shell")
    r = lax.axis_index("row")
    col = lax.axis_index("col")
    chips = rows // CORES
    h = r // CORES
    core = lax.rem(r, CORES)
    sibling = h * CORES + (CORES - 1 - core)
    points = right_ref.shape[1]
    width = right_ref.shape[2]
    tile_rows = left_ref.shape[1]
    own = tile_rows // shells
    pieces = own // chunk
    half = mult.shape[2]

    def places(sizes):
        return [(c, sum(sizes[:c]), size) for c, size in enumerate(sizes)]

    def parts(j):
        return places([chunk] * pieces)

    def bundles(j):
        return places([own - 2 * chunk, chunk, chunk] if j == shells - 1 else [own])

    bf16, f32 = jnp.bfloat16, jnp.float32

    slab = 256
    slabs = points // slab
    right_in = [
        pltpu.make_async_copy(
            right_hbm.at[:, pl.ds(b * slab, slab)], right_ref.at[:, pl.ds(b * slab, slab)], in_sem.at[b]
        )
        for b in range(slabs)
    ]
    left_in = pltpu.make_async_copy(left_hbm, left_ref, in_sem.at[slabs])
    inverse_in = pltpu.make_async_copy(inverse_hbm, inverse_ref, in_sem.at[slabs + 1])
    small_in = [
        pltpu.make_async_copy(source, target, in_sem.at[slabs + 2 + i])
        for i, (source, target) in enumerate([
            (point_hbm, point_ref), (shell_hbm, shell_ref), (green_hbm, green_ref), (pivot_hbm, pivot_ref)
        ])
    ]
    for copy in small_in[:3]:
        copy.start()
    right_in[0].start()
    left_in.start()
    for copy in right_in[1:]:
        copy.start()
    small_in[3].start()

    @pl.when(col == 0)
    def _():
        inverse_in.start()

    barrier = pltpu.get_barrier_semaphore()

    def greet(**where):
        pl.semaphore_signal(barrier, inc=1, device_id=where, device_id_type=MESH)

    for o in range(1, shells):
        greet(shell=lax.rem(s + o, shells))
    for d in range(1, chips):
        greet(row=lax.rem(h + d, chips) * CORES + core)
    greet(row=sibling)

    @pl.when(col > 0)
    def _():
        greet(col=col - 1)

    @pl.when(col < cols - 1)
    def _():
        greet(col=col + 1)

    for copy in small_in[:3]:
        copy.wait()
    count = green_ref.shape[1]
    padded = -(-count // 16) * 16
    index = shell_ref[...].reshape(1, points)
    match = lax.broadcasted_iota(jnp.int32, (padded, points), 0) == index

    def pieces_of(value):
        first = value.astype(bf16).astype(f32)
        second = (value - first).astype(bf16).astype(f32)
        return first, second, value - first - second

    hot = [jnp.where(match, piece, 0.0).astype(bf16) for piece in pieces_of(point_ref[...].reshape(1, points))]
    square = (padded, count)
    same = lax.broadcasted_iota(jnp.int32, square, 0) == lax.broadcasted_iota(jnp.int32, square, 1)
    table = jnp.concatenate(
        [
            jnp.broadcast_to(
                jnp.sum(
                    jnp.where(same, jnp.broadcast_to(green_ref[i : i + 1, :], square), 0.0),
                    axis=1, keepdims=True,
                ),
                (padded, 128),
            )
            for i in range(2)
        ],
        axis=1,
    )
    green = [piece.astype(bf16) for piece in pieces_of(table)]
    pairs = [(i, j) for i in range(3) for j in range(3 - i)]
    weights[...] = lax.dot_general(
        jnp.concatenate([hot[i] for i, _ in pairs], axis=0),
        jnp.concatenate([green[j] for _, j in pairs], axis=0),
        (((0,), (0,)), ((), ())),
        preferred_element_type=f32,
    )

    def span(first, size):
        return pl.ds(pl.multiple_of(first, math.gcd(size, chunk)), size)

    def y_copy(o, j, piece, group):
        c, start, size = piece
        at = span(group * own + start, size)
        return pltpu.make_async_remote_copy(
            src_ref=outgoing.at[at], dst_ref=incoming.at[o - 1, at],
            send_sem=y_send.at[o - 1, j, c], recv_sem=y_recv.at[o - 1, j, c],
            device_id={"shell": lax.rem(s + o, shells)}, device_id_type=MESH,
        )

    def x_copy(d, j, piece, group, row):
        c, start, size = piece
        at = span(row * tile_rows + group * own + start, size)
        return pltpu.make_async_remote_copy(
            src_ref=coupling.at[at], dst_ref=coupling.at[at],
            send_sem=x_send.at[d - 1, j, c], recv_sem=x_recv.at[d - 1, j, c],
            device_id={"row": lax.rem(h + d, chips) * CORES + core}, device_id_type=MESH,
        )

    def f_copy(d, j, piece, group, row):
        c, start, size = piece
        at = span(row * tile_rows + group * own + start, size)
        return pltpu.make_async_remote_copy(
            src_ref=coupling.at[at], dst_ref=coupling.at[at],
            send_sem=f_send.at[d, j, c], recv_sem=f_recv.at[d, j, c],
            device_id={"row": sibling}, device_id_type=MESH,
        )

    def m_copy(i):
        return pltpu.make_async_remote_copy(
            src_ref=mult.at[i], dst_ref=mult.at[i], send_sem=m_send.at[i], recv_sem=m_recv.at[i],
            device_id={"col": col + 1}, device_id_type=MESH,
        )

    def left_rows(group, at):
        rows_at = span(group * own, own)
        return jnp.concatenate([left_ref[0, rows_at, at], left_ref[1, rows_at, at]], axis=0)

    def combine(first_row, size):
        top = product[first_row : first_row + size, :]
        low = product[own + first_row : own + first_row + size, :]
        return top[:, :width] - low[:, width:], top[:, width:] + low[:, :width]

    first = lax.rem(s + 1, shells)
    for b in range(slabs):
        at = pl.ds(b * slab, slab)
        right_in[b].wait()
        w_real = jnp.concatenate([weights[at, :128]] * (width // 128), axis=1)
        w_imag = jnp.concatenate([weights[at, 128:]] * (width // 128), axis=1)
        b_real = right_ref[0, at, :].astype(f32)
        b_imag = right_ref[1, at, :].astype(f32)
        weighted[at, :width] = (w_real * b_real - w_imag * b_imag).astype(bf16)
        weighted[at, width:] = (w_real * b_imag + w_imag * b_real).astype(bf16)
        if b == 0:
            left_in.wait()
        term = jnp.dot(left_rows(first, at), weighted[at, :], preferred_element_type=f32)
        product[...] = term if b == 0 else product[...] + term

    for k in range(shells):
        group = lax.rem(s + 1 + k, shells)
        if k > 0:
            product[...] = jnp.dot(
                left_rows(group, pl.ds(0, points)), weighted[...], preferred_element_type=f32
            )
        if k == 0:
            line = jnp.minimum(col, 1) + jnp.minimum(cols - 1 - col, 1)
            pl.semaphore_wait(barrier, shells - 1 + chips + line)
        for o in range(1, shells):
            j = (1 + k - o) % shells
            for piece in parts(j):
                _, start, size = piece
                if o == 1:
                    at = span(group * own + start, size)
                    real, imag = combine(start, size)
                    part[at, :width] = real
                    part[at, width:] = imag
                    outgoing[at, :width] = real.astype(bf16)
                    outgoing[at, width:] = imag.astype(bf16)
                y_copy(o, j, piece, group).start()

    def choose(i):
        pivots = pivot_ref[...].reshape(1, -1)
        line = lax.broadcasted_iota(jnp.int32, (128, pivots.shape[1]), 0) + i * 128
        select[i * 128 : (i + 1) * 128, :] = jnp.where(line == pivots, 1.0, 0.0).astype(bf16)

    def forward(d, j, piece, group, row):
        for bundle in bundles(j):
            if piece[1] + piece[2] == bundle[1] + bundle[2]:
                f_copy(d, j, bundle, group, row).start()

    def take_y(j, piece):
        c, start, size = piece
        group = lax.rem(s + j, shells)
        at = span(group * own + start, size)
        total = part[at, :]
        for o in range(1, shells):
            y_copy(o, j, piece, group).wait_recv()
            total = total + incoming[o - 1, at, :].astype(f32)
        coupling[span(r * tile_rows + group * own + start, size), :] = total.astype(bf16)
        if j == 0:
            owned[start : start + size, :] = total
        for d in range(1, chips):
            x_copy(d, j, piece, group, r).start()
        forward(0, j, piece, group, r)
        if j == 0:

            @pl.when(col == 0)
            def _():
                if c == 0:
                    inverse_in.wait()
                batch = size
                panel = owned[start : start + size, :]
                high = panel.astype(bf16)
                low = (panel - high.astype(f32)).astype(bf16)
                four = jnp.concatenate(
                    [high[:, :width], low[:, :width], high[:, width:], low[:, width:]], axis=0
                )
                by_real = jnp.dot(four, inverse_ref[0], preferred_element_type=f32)
                by_imag = jnp.dot(four, inverse_ref[1], preferred_element_type=f32)

                def pick(value, at):
                    return value[at : at + batch] + value[at + batch : at + 2 * batch]

                m_real = (pick(by_real, 0) - pick(by_imag, 2 * batch)).astype(bf16)
                m_imag = (pick(by_imag, 0) + pick(by_real, 2 * batch)).astype(bf16)
                for p in range(size // half):
                    i = start // half + p
                    mult[i, 0] = m_real[p * half : (p + 1) * half]
                    mult[i, 1] = m_imag[p * half : (p + 1) * half]
                    if cols > 1:
                        m_copy(i).start()

    def take_x(j, piece):
        group = lax.rem(s + j, shells)
        for d in range(1, chips):
            row = lax.rem(h - d + chips, chips) * CORES + core
            x_copy(d, j, piece, group, row).wait_recv()
            forward(d, j, piece, group, row)

    passes = own // half

    def pass_mult(turn):
        for i in range(passes):
            k, odd = divmod(turn - i, 2)
            if odd == 0 and 0 < k < cols - 1:

                @pl.when(col == k)
                def _():
                    m_copy(i).wait_recv()
                    m_copy(i).start()

    def take_sibling(d, j):
        group = lax.rem(s + j, shells)
        row = lax.rem(h - d + chips, chips) * CORES + (CORES - 1 - core)
        for bundle in bundles(j):
            f_copy(d, j, bundle, group, row).wait_recv()

    steps = [(j, piece) for j in range(shells) for piece in parts(j)]
    lag = 2
    slices = select.shape[0] // 128
    small_in[3].wait()
    for n, (j, piece) in enumerate(steps):
        take_y(j, piece)
        pass_mult(n)
        if n >= lag:
            take_x(*steps[n - lag])
        for i in range(n * slices // len(steps), (n + 1) * slices // len(steps)):
            choose(i)

    for turn in range(len(steps), passes + 2 * cols):
        pass_mult(turn)

    for step in steps[-lag:-1]:
        take_x(*step)

    @pl.when((col == cols - 1) & (col > 0))
    def _():
        for i in range(passes):
            m_copy(i).wait_recv()

    factors = jnp.concatenate([mult[i, p] for p in range(2) for i in range(passes)], axis=0)
    spread[...] = lax.dot_general(
        factors, select[...], (((1,), (1,)), ((), ())), preferred_element_type=f32
    ).astype(bf16)
    for j in range(shells):
        take_sibling(0, j)
    near = span(h * CORES * tile_rows, CORES * tile_rows)
    product[...] = jnp.dot(spread[:, near], coupling[near, :], preferred_element_type=f32)
    for j in range(shells):
        if j == shells - 1:
            take_x(*steps[-1])
        group = lax.rem(s + j, shells)
        for d in range(1, chips):
            take_sibling(d, j)
            first_row = lax.rem(h - d + chips, chips) * CORES * tile_rows + group * own
            spots = [span(first_row + i * tile_rows, own) for i in range(CORES)]
            product[...] += jnp.dot(
                jnp.concatenate([spread[:, at] for at in spots], axis=1),
                jnp.concatenate([coupling[at, :] for at in spots], axis=0),
                preferred_element_type=f32,
            )
    real, imag = combine(0, own)
    out_ref[0, 0, 0] = owned[:, :width] - real
    out_ref[1, 0, 0] = owned[:, width:] - imag

    for j in range(shells):
        group = lax.rem(s + j, shells)
        for piece in parts(j):
            for o in range(1, shells):
                k = (j + o - 1) % shells
                y_copy(o, j, piece, lax.rem(s + 1 + k, shells)).wait_send()
            for d in range(1, chips):
                x_copy(d, j, piece, group, r).wait_send()
        for bundle in bundles(j):
            f_copy(0, j, bundle, group, r).wait_send()
            for d in range(1, chips):
                f_copy(d, j, bundle, group, lax.rem(h - d + chips, chips) * CORES + core).wait_send()

    @pl.when(col < cols - 1)
    def _():
        for i in range(passes):
            m_copy(i).wait_send()


def body(sizes, left_basis, right_basis, point_weight, shell_index, green_table, pivot_rows, diag_inverse):
    shells, rows, cols = sizes
    chips = rows // CORES
    tile_rows, points = left_basis.shape[1:]
    width = right_basis.shape[2]
    own = tile_rows // shells
    chunk = own // 4
    half = chunk
    pieces = own // chunk
    all_rows = rows * tile_rows
    bf16, f32 = jnp.bfloat16, jnp.float32
    vmem = pl.BlockSpec(memory_space=pltpu.VMEM)
    sems = pltpu.SemaphoreType.DMA
    buffers = [
        ((2, tile_rows, points), bf16),
        ((2, points, width), bf16),
        (diag_inverse.shape, bf16),
        (point_weight.shape, f32),
        (shell_index.shape, jnp.int32),
        (green_table.shape[::-1], f32),
        (pivot_rows.shape, jnp.int32),
        ((points, 256), f32),
        ((points, 2 * width), bf16),
        ((2 * own, 2 * width), f32),
        ((tile_rows, 2 * width), f32),
        ((tile_rows, 2 * width), bf16),
        ((max(shells - 1, 1), tile_rows, 2 * width), bf16),
        ((all_rows, 2 * width), bf16),
        ((own, 2 * width), f32),
        ((own // half, 2, half, width), bf16),
        ((all_rows, pivot_rows.shape[0]), bf16),
        ((2 * own, all_rows), bf16),
    ]
    held = sum(math.prod(shape) * jnp.dtype(kind).itemsize for shape, kind in buffers)
    return pl.pallas_call(
        functools.partial(kernel, shells, rows, cols, chunk),
        out_shape=pltpu.VMEM((2, 1, 1, own, width), f32),
        in_specs=[pl.BlockSpec(memory_space=pltpu.HBM)] * 7,
        out_specs=vmem,
        scratch_shapes=[pltpu.VMEM(shape, kind) for shape, kind in buffers] + [
            sems((points // 256 + 6,)),
            sems((max(shells - 1, 1), shells, pieces)),
            sems((max(shells - 1, 1), shells, pieces)),
            sems((max(chips - 1, 1), shells, pieces)),
            sems((max(chips - 1, 1), shells, pieces)),
            sems((chips, shells, pieces)),
            sems((chips, shells, pieces)),
            sems((own // half,)),
            sems((own // half,)),
        ],
        compiler_params=pltpu.CompilerParams(
            collective_id=0, has_side_effects=True, vmem_limit_bytes=56 * 2**20
        ),
        cost_estimate=pl.CostEstimate(
            flops=2 * tile_rows * 2 * points * 2 * width + 4 * own * all_rows * 2 * width,
            bytes_accessed=8 * 2**20,
            transcendentals=0,
        ),
    )(left_basis, right_basis, point_weight, shell_index, green_table.T, pivot_rows, diag_inverse)


def solution(mesh):
    sizes = tuple(mesh.shape[name] for name in ("shell", "row", "col"))
    return jax.shard_map(
        functools.partial(body, sizes),
        mesh=mesh,
        in_specs=(
            P(None, "row", "shell"),
            P(None, "shell", "col"),
            P("shell"),
            P("shell"),
            P(),
            P(),
            P(),
        ),
        out_specs=P(None, "row", "shell", None, "col"),
        check_vma=False,
    )
```

```python
import functools
import math
import jax
import jax.numpy as jnp
from jax import lax
from jax.experimental import pallas as pl
from jax.experimental.pallas import tpu as pltpu
from jax.sharding import PartitionSpec as P

MESH = pl.DeviceIdType.MESH
CORES = 2


def kernel(shells, rows, cols, chunk, left_hbm, right_hbm, point_hbm, shell_hbm, green_hbm, pivot_hbm,
           inverse_hbm, out_ref, left_ref, right_ref, inverse_ref, point_ref, shell_ref, green_ref, pivot_ref, weights, weighted, product, part,
           outgoing, incoming, coupling, owned, mult, select, spread, in_sem, y_send, y_recv, x_send,
           x_recv, f_send, f_recv, m_send, m_recv):
    s = lax.axis_index("shell")
    r = lax.axis_index("row")
    col = lax.axis_index("col")
    chips = rows // CORES
    h = r // CORES
    core = lax.rem(r, CORES)
    sibling = h * CORES + (CORES - 1 - core)
    points = right_ref.shape[1]
    width = right_ref.shape[2]
    tile_rows = left_ref.shape[1]
    own = tile_rows // shells
    half = mult.shape[2]

    def places(sizes):
        return [(c, sum(sizes[:c]), size) for c, size in enumerate(sizes)]

    def parts(j):
        short = [chunk // 2] * 2 if j == shells - 1 else [chunk]
        return places([chunk] * (own // chunk - 1) + short)

    def bundles(j):
        return places([own - chunk] + [chunk // 2] * 2 if j == shells - 1 else [own])

    bf16, f32 = jnp.bfloat16, jnp.float32

    slab = 256
    slabs = points // slab
    right_in = [
        pltpu.make_async_copy(
            right_hbm.at[:, pl.ds(b * slab, slab)], right_ref.at[:, pl.ds(b * slab, slab)], in_sem.at[b]
        )
        for b in range(slabs)
    ]
    left_in = pltpu.make_async_copy(left_hbm, left_ref, in_sem.at[slabs])
    inverse_in = pltpu.make_async_copy(inverse_hbm, inverse_ref, in_sem.at[slabs + 1])
    small_in = [
        pltpu.make_async_copy(source, target, in_sem.at[slabs + 2 + i])
        for i, (source, target) in enumerate([
            (point_hbm, point_ref), (shell_hbm, shell_ref), (green_hbm, green_ref), (pivot_hbm, pivot_ref)
        ])
    ]
    for copy in small_in[:3]:
        copy.start()
    right_in[0].start()
    left_in.start()
    for copy in right_in[1:]:
        copy.start()
    small_in[3].start()

    @pl.when(col == 0)
    def _():
        inverse_in.start()

    barrier = pltpu.get_barrier_semaphore()

    def greet(**where):
        pl.semaphore_signal(barrier, inc=1, device_id=where, device_id_type=MESH)

    for o in range(1, shells):
        greet(shell=lax.rem(s + o, shells))
    for d in range(1, chips):
        greet(row=lax.rem(h + d, chips) * CORES + core)
    greet(row=sibling)

    @pl.when(col > 0)
    def _():
        greet(col=col - 1)

    @pl.when(col < cols - 1)
    def _():
        greet(col=col + 1)

    for copy in small_in[:3]:
        copy.wait()
    count = green_ref.shape[1]
    padded = -(-count // 16) * 16
    index = shell_ref[...].reshape(1, points)
    match = lax.broadcasted_iota(jnp.int32, (padded, points), 0) == index

    def pieces_of(value):
        first = value.astype(bf16).astype(f32)
        second = (value - first).astype(bf16).astype(f32)
        return first, second, value - first - second

    hot = [jnp.where(match, piece, 0.0).astype(bf16) for piece in pieces_of(point_ref[...].reshape(1, points))]
    square = (padded, count)
    same = lax.broadcasted_iota(jnp.int32, square, 0) == lax.broadcasted_iota(jnp.int32, square, 1)
    table = jnp.concatenate(
        [
            jnp.broadcast_to(
                jnp.sum(
                    jnp.where(same, jnp.broadcast_to(green_ref[i : i + 1, :], square), 0.0),
                    axis=1, keepdims=True,
                ),
                (padded, 128),
            )
            for i in range(2)
        ],
        axis=1,
    )
    green = [piece.astype(bf16) for piece in pieces_of(table)]
    pairs = [(i, j) for i in range(3) for j in range(3 - i)]
    weights[...] = lax.dot_general(
        jnp.concatenate([hot[i] for i, _ in pairs], axis=0),
        jnp.concatenate([green[j] for _, j in pairs], axis=0),
        (((0,), (0,)), ((), ())),
        preferred_element_type=f32,
    )

    def span(first, size):
        return pl.ds(pl.multiple_of(first, math.gcd(size, chunk)), size)

    def y_copy(o, j, piece, group):
        c, start, size = piece
        at = span(group * own + start, size)
        return pltpu.make_async_remote_copy(
            src_ref=outgoing.at[at], dst_ref=incoming.at[o - 1, at],
            send_sem=y_send.at[o - 1, j, c], recv_sem=y_recv.at[o - 1, j, c],
            device_id={"shell": lax.rem(s + o, shells)}, device_id_type=MESH,
        )

    def x_copy(d, j, piece, group, row):
        c, start, size = piece
        at = span(row * tile_rows + group * own + start, size)
        return pltpu.make_async_remote_copy(
            src_ref=coupling.at[at], dst_ref=coupling.at[at],
            send_sem=x_send.at[d - 1, j, c], recv_sem=x_recv.at[d - 1, j, c],
            device_id={"row": lax.rem(h + d, chips) * CORES + core}, device_id_type=MESH,
        )

    def f_copy(d, j, piece, group, row):
        c, start, size = piece
        at = span(row * tile_rows + group * own + start, size)
        return pltpu.make_async_remote_copy(
            src_ref=coupling.at[at], dst_ref=coupling.at[at],
            send_sem=f_send.at[d, j, c], recv_sem=f_recv.at[d, j, c],
            device_id={"row": sibling}, device_id_type=MESH,
        )

    def m_copy(i):
        return pltpu.make_async_remote_copy(
            src_ref=mult.at[i], dst_ref=mult.at[i], send_sem=m_send.at[i], recv_sem=m_recv.at[i],
            device_id={"col": col + 1}, device_id_type=MESH,
        )

    def left_rows(group, at):
        rows_at = span(group * own, own)
        return jnp.concatenate([left_ref[0, rows_at, at], left_ref[1, rows_at, at]], axis=0)

    def combine(first_row, size):
        top = product[first_row : first_row + size, :]
        low = product[own + first_row : own + first_row + size, :]
        return top[:, :width] - low[:, width:], top[:, width:] + low[:, :width]

    first = lax.rem(s + 1, shells)
    for b in range(slabs):
        at = pl.ds(b * slab, slab)
        right_in[b].wait()
        w_real = jnp.concatenate([weights[at, :128]] * (width // 128), axis=1)
        w_imag = jnp.concatenate([weights[at, 128:]] * (width // 128), axis=1)
        b_real = right_ref[0, at, :].astype(f32)
        b_imag = right_ref[1, at, :].astype(f32)
        weighted[at, :width] = (w_real * b_real - w_imag * b_imag).astype(bf16)
        weighted[at, width:] = (w_real * b_imag + w_imag * b_real).astype(bf16)
        if b == 0:
            left_in.wait()
        term = jnp.dot(left_rows(first, at), weighted[at, :], preferred_element_type=f32)
        product[...] = term if b == 0 else product[...] + term

    for k in range(shells):
        group = lax.rem(s + 1 + k, shells)
        if k > 0:
            product[...] = jnp.dot(
                left_rows(group, pl.ds(0, points)), weighted[...], preferred_element_type=f32
            )
        if k == 0:
            line = jnp.minimum(col, 1) + jnp.minimum(cols - 1 - col, 1)
            pl.semaphore_wait(barrier, shells - 1 + chips + line)
        for o in range(1, shells):
            j = (1 + k - o) % shells
            for piece in parts(j):
                _, start, size = piece
                if o == 1:
                    at = span(group * own + start, size)
                    real, imag = combine(start, size)
                    part[at, :width] = real
                    part[at, width:] = imag
                    outgoing[at, :width] = real.astype(bf16)
                    outgoing[at, width:] = imag.astype(bf16)
                y_copy(o, j, piece, group).start()

    def choose(i):
        pivots = pivot_ref[...].reshape(1, -1)
        line = lax.broadcasted_iota(jnp.int32, (128, pivots.shape[1]), 0) + i * 128
        select[i * 128 : (i + 1) * 128, :] = jnp.where(line == pivots, 1.0, 0.0).astype(bf16)

    def forward(d, j, piece, group, row):
        for bundle in bundles(j):
            if piece[1] + piece[2] == bundle[1] + bundle[2]:
                f_copy(d, j, bundle, group, row).start()

    def take_y(j, piece):
        c, start, size = piece
        group = lax.rem(s + j, shells)
        at = span(group * own + start, size)
        total = part[at, :]
        for o in range(1, shells):
            y_copy(o, j, piece, group).wait_recv()
            total = total + incoming[o - 1, at, :].astype(f32)
        coupling[span(r * tile_rows + group * own + start, size), :] = total.astype(bf16)
        if j == 0:
            owned[start : start + size, :] = total
        for d in range(1, chips):
            x_copy(d, j, piece, group, r).start()
        forward(0, j, piece, group, r)
        if j == 0:

            @pl.when(col == 0)
            def _():
                if c == 0:
                    inverse_in.wait()
                batch = size
                panel = owned[start : start + size, :]
                high = panel.astype(bf16)
                low = (panel - high.astype(f32)).astype(bf16)
                four = jnp.concatenate(
                    [high[:, :width], low[:, :width], high[:, width:], low[:, width:]], axis=0
                )
                by_real = jnp.dot(four, inverse_ref[0], preferred_element_type=f32)
                by_imag = jnp.dot(four, inverse_ref[1], preferred_element_type=f32)

                def pick(value, at):
                    return value[at : at + batch] + value[at + batch : at + 2 * batch]

                m_real = (pick(by_real, 0) - pick(by_imag, 2 * batch)).astype(bf16)
                m_imag = (pick(by_imag, 0) + pick(by_real, 2 * batch)).astype(bf16)
                for p in range(size // half):
                    i = start // half + p
                    mult[i, 0] = m_real[p * half : (p + 1) * half]
                    mult[i, 1] = m_imag[p * half : (p + 1) * half]
                    if cols > 1:
                        m_copy(i).start()

    def take_x(j, piece):
        group = lax.rem(s + j, shells)
        for d in range(1, chips):
            row = lax.rem(h - d + chips, chips) * CORES + core
            x_copy(d, j, piece, group, row).wait_recv()
            forward(d, j, piece, group, row)

    passes = own // half

    def pass_mult(turn):
        for i in range(passes):
            k = turn - 1 - i * half // chunk
            if 0 < k < cols - 1:

                @pl.when(col == k)
                def _():
                    m_copy(i).wait_recv()
                    m_copy(i).start()

    def take_sibling(d, j):
        group = lax.rem(s + j, shells)
        row = lax.rem(h - d + chips, chips) * CORES + (CORES - 1 - core)
        for bundle in bundles(j):
            f_copy(d, j, bundle, group, row).wait_recv()

    steps = [(j, piece) for j in range(shells) for piece in parts(j)]
    lag = 2
    slices = select.shape[0] // 128
    small_in[3].wait()
    for n, (j, piece) in enumerate(steps):
        take_y(j, piece)
        pass_mult(n)
        if n >= lag:
            take_x(*steps[n - lag])
        for i in range(n * slices // len(steps), (n + 1) * slices // len(steps)):
            choose(i)

    for turn in range(len(steps), passes + cols):
        pass_mult(turn)

    for step in steps[-lag:-1]:
        take_x(*step)

    @pl.when((col == cols - 1) & (col > 0))
    def _():
        for i in range(passes):
            m_copy(i).wait_recv()

    factors = jnp.concatenate([mult[i, p] for p in range(2) for i in range(passes)], axis=0)
    spread[...] = lax.dot_general(
        factors, select[...], (((1,), (1,)), ((), ())), preferred_element_type=f32
    ).astype(bf16)
    for j in range(shells):
        take_sibling(0, j)
    near = span(h * CORES * tile_rows, CORES * tile_rows)
    product[...] = jnp.dot(spread[:, near], coupling[near, :], preferred_element_type=f32)
    for j in range(shells):
        if j == shells - 1:
            take_x(*steps[-1])
        group = lax.rem(s + j, shells)
        for d in range(1, chips):
            take_sibling(d, j)
            first_row = lax.rem(h - d + chips, chips) * CORES * tile_rows + group * own
            spots = [span(first_row + i * tile_rows, own) for i in range(CORES)]
            product[...] += jnp.dot(
                jnp.concatenate([spread[:, at] for at in spots], axis=1),
                jnp.concatenate([coupling[at, :] for at in spots], axis=0),
                preferred_element_type=f32,
            )
    real, imag = combine(0, own)
    out_ref[0, 0, 0] = owned[:, :width] - real
    out_ref[1, 0, 0] = owned[:, width:] - imag

    for j in range(shells):
        group = lax.rem(s + j, shells)
        for piece in parts(j):
            for o in range(1, shells):
                k = (j + o - 1) % shells
                y_copy(o, j, piece, lax.rem(s + 1 + k, shells)).wait_send()
            for d in range(1, chips):
                x_copy(d, j, piece, group, r).wait_send()
        for bundle in bundles(j):
            f_copy(0, j, bundle, group, r).wait_send()
            for d in range(1, chips):
                f_copy(d, j, bundle, group, lax.rem(h - d + chips, chips) * CORES + core).wait_send()

    @pl.when(col < cols - 1)
    def _():
        for i in range(passes):
            m_copy(i).wait_send()


def body(sizes, left_basis, right_basis, point_weight, shell_index, green_table, pivot_rows, diag_inverse):
    shells, rows, cols = sizes
    chips = rows // CORES
    tile_rows, points = left_basis.shape[1:]
    width = right_basis.shape[2]
    own = tile_rows // shells
    chunk = own // 4
    half = chunk // 2
    pieces = own // chunk + 1
    all_rows = rows * tile_rows
    bf16, f32 = jnp.bfloat16, jnp.float32
    vmem = pl.BlockSpec(memory_space=pltpu.VMEM)
    sems = pltpu.SemaphoreType.DMA
    buffers = [
        ((2, tile_rows, points), bf16),
        ((2, points, width), bf16),
        (diag_inverse.shape, bf16),
        (point_weight.shape, f32),
        (shell_index.shape, jnp.int32),
        (green_table.shape[::-1], f32),
        (pivot_rows.shape, jnp.int32),
        ((points, 256), f32),
        ((points, 2 * width), bf16),
        ((2 * own, 2 * width), f32),
        ((tile_rows, 2 * width), f32),
        ((tile_rows, 2 * width), bf16),
        ((max(shells - 1, 1), tile_rows, 2 * width), bf16),
        ((all_rows, 2 * width), bf16),
        ((own, 2 * width), f32),
        ((own // half, 2, half, width), bf16),
        ((all_rows, pivot_rows.shape[0]), bf16),
        ((2 * own, all_rows), bf16),
    ]
    held = sum(math.prod(shape) * jnp.dtype(kind).itemsize for shape, kind in buffers)
    return pl.pallas_call(
        functools.partial(kernel, shells, rows, cols, chunk),
        out_shape=pltpu.VMEM((2, 1, 1, own, width), f32),
        in_specs=[pl.BlockSpec(memory_space=pltpu.HBM)] * 7,
        out_specs=vmem,
        scratch_shapes=[pltpu.VMEM(shape, kind) for shape, kind in buffers] + [
            sems((points // 256 + 6,)),
            sems((max(shells - 1, 1), shells, pieces)),
            sems((max(shells - 1, 1), shells, pieces)),
            sems((max(chips - 1, 1), shells, pieces)),
            sems((max(chips - 1, 1), shells, pieces)),
            sems((chips, shells, pieces)),
            sems((chips, shells, pieces)),
            sems((own // half,)),
            sems((own // half,)),
        ],
        compiler_params=pltpu.CompilerParams(
            collective_id=0, has_side_effects=True, vmem_limit_bytes=56 * 2**20
        ),
        cost_estimate=pl.CostEstimate(
            flops=2 * tile_rows * 2 * points * 2 * width + 4 * own * all_rows * 2 * width,
            bytes_accessed=8 * 2**20,
            transcendentals=0,
        ),
    )(left_basis, right_basis, point_weight, shell_index, green_table.T, pivot_rows, diag_inverse)


def solution(mesh):
    sizes = tuple(mesh.shape[name] for name in ("shell", "row", "col"))
    return jax.shard_map(
        functools.partial(body, sizes),
        mesh=mesh,
        in_specs=(
            P(None, "row", "shell"),
            P(None, "shell", "col"),
            P("shell"),
            P("shell"),
            P(),
            P(),
            P(),
        ),
        out_specs=P(None, "row", "shell", None, "col"),
        check_vma=False,
    )
```

```python
import functools
import math
import jax
import jax.numpy as jnp
from jax import lax
from jax.experimental import pallas as pl
from jax.experimental.pallas import tpu as pltpu
from jax.sharding import PartitionSpec as P

MESH = pl.DeviceIdType.MESH
CORES = 2


def kernel(shells, rows, cols, chunk, left_hbm, right_hbm, point_hbm, shell_hbm, green_hbm, pivot_hbm,
           inverse_hbm, out_ref, left_ref, right_ref, inverse_ref, point_ref, shell_ref, green_ref, pivot_ref, weights, weighted, product, part,
           outgoing, incoming, coupling, owned, mult, select, spread, in_sem, y_send, y_recv, x_send,
           x_recv, f_send, f_recv, m_send, m_recv):
    s = lax.axis_index("shell")
    r = lax.axis_index("row")
    col = lax.axis_index("col")
    chips = rows // CORES
    h = r // CORES
    core = lax.rem(r, CORES)
    sibling = h * CORES + (CORES - 1 - core)
    points = right_ref.shape[1]
    width = right_ref.shape[2]
    tile_rows = left_ref.shape[1]
    own = tile_rows // shells
    pieces = own // chunk
    half = mult.shape[2]

    def places(sizes):
        return [(c, sum(sizes[:c]), size) for c, size in enumerate(sizes)]

    def parts(j):
        return places([own - 2 * chunk, chunk, chunk] if j == shells - 1 else [chunk] * pieces)

    def bundles(j):
        return parts(j) if j == shells - 1 else [(0, 0, own)]

    bf16, f32 = jnp.bfloat16, jnp.float32

    slab = 256
    slabs = points // slab
    right_in = [
        pltpu.make_async_copy(
            right_hbm.at[:, pl.ds(b * slab, slab)], right_ref.at[:, pl.ds(b * slab, slab)], in_sem.at[b]
        )
        for b in range(slabs)
    ]
    left_in = pltpu.make_async_copy(left_hbm, left_ref, in_sem.at[slabs])
    inverse_in = pltpu.make_async_copy(inverse_hbm, inverse_ref, in_sem.at[slabs + 1])
    small_in = [
        pltpu.make_async_copy(source, target, in_sem.at[slabs + 2 + i])
        for i, (source, target) in enumerate([
            (point_hbm, point_ref), (shell_hbm, shell_ref), (green_hbm, green_ref), (pivot_hbm, pivot_ref)
        ])
    ]
    for copy in small_in[:3]:
        copy.start()
    right_in[0].start()
    left_in.start()
    for copy in right_in[1:]:
        copy.start()
    small_in[3].start()

    @pl.when(col == 0)
    def _():
        inverse_in.start()

    barrier = pltpu.get_barrier_semaphore()

    def greet(**where):
        pl.semaphore_signal(barrier, inc=1, device_id=where, device_id_type=MESH)

    for o in range(1, shells):
        greet(shell=lax.rem(s + o, shells))
    for d in range(1, chips):
        greet(row=lax.rem(h + d, chips) * CORES + core)
    greet(row=sibling)

    @pl.when(col > 0)
    def _():
        greet(col=col - 1)

    @pl.when(col < cols - 1)
    def _():
        greet(col=col + 1)

    for copy in small_in[:3]:
        copy.wait()
    count = green_ref.shape[1]
    padded = -(-count // 16) * 16
    index = shell_ref[...].reshape(1, points)
    match = lax.broadcasted_iota(jnp.int32, (padded, points), 0) == index

    def pieces_of(value):
        first = value.astype(bf16).astype(f32)
        second = (value - first).astype(bf16).astype(f32)
        return first, second, value - first - second

    hot = [jnp.where(match, piece, 0.0).astype(bf16) for piece in pieces_of(point_ref[...].reshape(1, points))]
    square = (padded, count)
    same = lax.broadcasted_iota(jnp.int32, square, 0) == lax.broadcasted_iota(jnp.int32, square, 1)
    table = jnp.concatenate(
        [
            jnp.broadcast_to(
                jnp.sum(
                    jnp.where(same, jnp.broadcast_to(green_ref[i : i + 1, :], square), 0.0),
                    axis=1, keepdims=True,
                ),
                (padded, 128),
            )
            for i in range(2)
        ],
        axis=1,
    )
    green = [piece.astype(bf16) for piece in pieces_of(table)]
    pairs = [(i, j) for i in range(3) for j in range(3 - i)]
    weights[...] = lax.dot_general(
        jnp.concatenate([hot[i] for i, _ in pairs], axis=0),
        jnp.concatenate([green[j] for _, j in pairs], axis=0),
        (((0,), (0,)), ((), ())),
        preferred_element_type=f32,
    )

    def span(first, size):
        return pl.ds(pl.multiple_of(first, math.gcd(size, chunk)), size)

    def y_copy(o, j, piece, group):
        c, start, size = piece
        at = span(group * own + start, size)
        return pltpu.make_async_remote_copy(
            src_ref=outgoing.at[at], dst_ref=incoming.at[o - 1, at],
            send_sem=y_send.at[o - 1, j, c], recv_sem=y_recv.at[o - 1, j, c],
            device_id={"shell": lax.rem(s + o, shells)}, device_id_type=MESH,
        )

    def x_copy(d, j, piece, group, row):
        c, start, size = piece
        at = span(row * tile_rows + group * own + start, size)
        return pltpu.make_async_remote_copy(
            src_ref=coupling.at[at], dst_ref=coupling.at[at],
            send_sem=x_send.at[d - 1, j, c], recv_sem=x_recv.at[d - 1, j, c],
            device_id={"row": lax.rem(h + d, chips) * CORES + core}, device_id_type=MESH,
        )

    def f_copy(d, j, piece, group, row):
        c, start, size = piece
        at = span(row * tile_rows + group * own + start, size)
        return pltpu.make_async_remote_copy(
            src_ref=coupling.at[at], dst_ref=coupling.at[at],
            send_sem=f_send.at[d, j, c], recv_sem=f_recv.at[d, j, c],
            device_id={"row": sibling}, device_id_type=MESH,
        )

    def m_copy(i):
        return pltpu.make_async_remote_copy(
            src_ref=mult.at[i], dst_ref=mult.at[i], send_sem=m_send.at[i], recv_sem=m_recv.at[i],
            device_id={"col": col + 1}, device_id_type=MESH,
        )

    def left_rows(group, at):
        rows_at = span(group * own, own)
        return jnp.concatenate([left_ref[0, rows_at, at], left_ref[1, rows_at, at]], axis=0)

    def combine(first_row, size):
        top = product[first_row : first_row + size, :]
        low = product[own + first_row : own + first_row + size, :]
        return top[:, :width] - low[:, width:], top[:, width:] + low[:, :width]

    first = lax.rem(s + 1, shells)
    for b in range(slabs):
        at = pl.ds(b * slab, slab)
        right_in[b].wait()
        w_real = jnp.concatenate([weights[at, :128]] * (width // 128), axis=1)
        w_imag = jnp.concatenate([weights[at, 128:]] * (width // 128), axis=1)
        b_real = right_ref[0, at, :].astype(f32)
        b_imag = right_ref[1, at, :].astype(f32)
        weighted[at, :width] = (w_real * b_real - w_imag * b_imag).astype(bf16)
        weighted[at, width:] = (w_real * b_imag + w_imag * b_real).astype(bf16)
        if b == 0:
            left_in.wait()
        term = jnp.dot(left_rows(first, at), weighted[at, :], preferred_element_type=f32)
        product[...] = term if b == 0 else product[...] + term

    for k in range(shells):
        group = lax.rem(s + 1 + k, shells)
        if k > 0:
            product[...] = jnp.dot(
                left_rows(group, pl.ds(0, points)), weighted[...], preferred_element_type=f32
            )
        if k == 0:
            line = jnp.minimum(col, 1) + jnp.minimum(cols - 1 - col, 1)
            pl.semaphore_wait(barrier, shells - 1 + chips + line)
        for o in range(1, shells):
            j = (1 + k - o) % shells
            for piece in parts(j):
                _, start, size = piece
                if o == 1:
                    at = span(group * own + start, size)
                    real, imag = combine(start, size)
                    part[at, :width] = real
                    part[at, width:] = imag
                    outgoing[at, :width] = real.astype(bf16)
                    outgoing[at, width:] = imag.astype(bf16)
                y_copy(o, j, piece, group).start()

    def choose(i):
        pivots = pivot_ref[...].reshape(1, -1)
        line = lax.broadcasted_iota(jnp.int32, (128, pivots.shape[1]), 0) + i * 128
        select[i * 128 : (i + 1) * 128, :] = jnp.where(line == pivots, 1.0, 0.0).astype(bf16)

    def forward(d, j, piece, group, row):
        for bundle in bundles(j):
            if piece[1] + piece[2] == bundle[1] + bundle[2]:
                f_copy(d, j, bundle, group, row).start()

    def take_y(j, piece):
        c, start, size = piece
        group = lax.rem(s + j, shells)
        at = span(group * own + start, size)
        total = part[at, :]
        for o in range(1, shells):
            y_copy(o, j, piece, group).wait_recv()
            total = total + incoming[o - 1, at, :].astype(f32)
        coupling[span(r * tile_rows + group * own + start, size), :] = total.astype(bf16)
        if j == 0:
            owned[start : start + size, :] = total
        for d in range(1, chips):
            x_copy(d, j, piece, group, r).start()
        forward(0, j, piece, group, r)
        if j == 0:

            @pl.when(col == 0)
            def _():
                if c == 0:
                    inverse_in.wait()
                batch = size
                panel = owned[start : start + size, :]
                high = panel.astype(bf16)
                low = (panel - high.astype(f32)).astype(bf16)
                four = jnp.concatenate(
                    [high[:, :width], low[:, :width], high[:, width:], low[:, width:]], axis=0
                )
                by_real = jnp.dot(four, inverse_ref[0], preferred_element_type=f32)
                by_imag = jnp.dot(four, inverse_ref[1], preferred_element_type=f32)

                def pick(value, at):
                    return value[at : at + batch] + value[at + batch : at + 2 * batch]

                m_real = (pick(by_real, 0) - pick(by_imag, 2 * batch)).astype(bf16)
                m_imag = (pick(by_imag, 0) + pick(by_real, 2 * batch)).astype(bf16)
                for p in range(size // half):
                    i = start // half + p
                    mult[i, 0] = m_real[p * half : (p + 1) * half]
                    mult[i, 1] = m_imag[p * half : (p + 1) * half]
                    if cols > 1:
                        m_copy(i).start()

    def take_x(j, piece):
        group = lax.rem(s + j, shells)
        for d in range(1, chips):
            row = lax.rem(h - d + chips, chips) * CORES + core
            x_copy(d, j, piece, group, row).wait_recv()
            forward(d, j, piece, group, row)

    passes = own // half

    ends = [j * own + start + size for j in range(shells) for _, start, size in parts(j)]

    def turn_of(i, k):
        rows_by_then = (2 * i + 4 + 3 * k) * half // 2
        late = [n for n in range(len(ends) - 1) if ends[n + 1] >= rows_by_then]
        return late[0] if late else len(ends)

    def pass_mult(turn):
        for k in range(1, cols - 1):
            for i in range(passes):
                if turn == turn_of(i, k):

                    @pl.when(col == k)
                    def _():
                        m_copy(i).wait_recv()
                        m_copy(i).start()

    def take_sibling(d, j):
        group = lax.rem(s + j, shells)
        row = lax.rem(h - d + chips, chips) * CORES + (CORES - 1 - core)
        for bundle in bundles(j):
            f_copy(d, j, bundle, group, row).wait_recv()

    steps = [(j, piece) for j in range(shells) for piece in parts(j)]
    lag = 2
    slices = select.shape[0] // 128
    small_in[3].wait()
    for n, (j, piece) in enumerate(steps):
        take_y(j, piece)
        pass_mult(n)
        if n >= lag:
            take_x(*steps[n - lag])
        for i in range(n * slices // len(steps), (n + 1) * slices // len(steps)):
            choose(i)

    pass_mult(len(steps))

    for step in steps[-lag:-1]:
        take_x(*step)

    @pl.when((col == cols - 1) & (col > 0))
    def _():
        for i in range(passes):
            m_copy(i).wait_recv()

    factors = jnp.concatenate([mult[i, p] for p in range(2) for i in range(passes)], axis=0)
    spread[...] = lax.dot_general(
        factors, select[...], (((1,), (1,)), ((), ())), preferred_element_type=f32
    ).astype(bf16)
    for j in range(shells):
        take_sibling(0, j)
    near = span(h * CORES * tile_rows, CORES * tile_rows)
    product[...] = jnp.dot(spread[:, near], coupling[near, :], preferred_element_type=f32)
    for j in range(shells):
        if j == shells - 1:
            take_x(*steps[-1])
        group = lax.rem(s + j, shells)
        for d in range(1, chips):
            take_sibling(d, j)
            first_row = lax.rem(h - d + chips, chips) * CORES * tile_rows + group * own
            spots = [span(first_row + i * tile_rows, own) for i in range(CORES)]
            product[...] += jnp.dot(
                jnp.concatenate([spread[:, at] for at in spots], axis=1),
                jnp.concatenate([coupling[at, :] for at in spots], axis=0),
                preferred_element_type=f32,
            )
    real, imag = combine(0, own)
    out_ref[0, 0, 0] = owned[:, :width] - real
    out_ref[1, 0, 0] = owned[:, width:] - imag

    for j in range(shells):
        group = lax.rem(s + j, shells)
        for piece in parts(j):
            for o in range(1, shells):
                k = (j + o - 1) % shells
                y_copy(o, j, piece, lax.rem(s + 1 + k, shells)).wait_send()
            for d in range(1, chips):
                x_copy(d, j, piece, group, r).wait_send()
        for bundle in bundles(j):
            f_copy(0, j, bundle, group, r).wait_send()
            for d in range(1, chips):
                f_copy(d, j, bundle, group, lax.rem(h - d + chips, chips) * CORES + core).wait_send()

    @pl.when(col < cols - 1)
    def _():
        for i in range(passes):
            m_copy(i).wait_send()


def body(sizes, left_basis, right_basis, point_weight, shell_index, green_table, pivot_rows, diag_inverse):
    shells, rows, cols = sizes
    chips = rows // CORES
    tile_rows, points = left_basis.shape[1:]
    width = right_basis.shape[2]
    own = tile_rows // shells
    chunk = own // 4
    half = chunk
    pieces = own // chunk
    all_rows = rows * tile_rows
    bf16, f32 = jnp.bfloat16, jnp.float32
    vmem = pl.BlockSpec(memory_space=pltpu.VMEM)
    sems = pltpu.SemaphoreType.DMA
    buffers = [
        ((2, tile_rows, points), bf16),
        ((2, points, width), bf16),
        (diag_inverse.shape, bf16),
        (point_weight.shape, f32),
        (shell_index.shape, jnp.int32),
        (green_table.shape[::-1], f32),
        (pivot_rows.shape, jnp.int32),
        ((points, 256), f32),
        ((points, 2 * width), bf16),
        ((2 * own, 2 * width), f32),
        ((tile_rows, 2 * width), f32),
        ((tile_rows, 2 * width), bf16),
        ((max(shells - 1, 1), tile_rows, 2 * width), bf16),
        ((all_rows, 2 * width), bf16),
        ((own, 2 * width), f32),
        ((own // half, 2, half, width), bf16),
        ((all_rows, pivot_rows.shape[0]), bf16),
        ((2 * own, all_rows), bf16),
    ]
    held = sum(math.prod(shape) * jnp.dtype(kind).itemsize for shape, kind in buffers)
    return pl.pallas_call(
        functools.partial(kernel, shells, rows, cols, chunk),
        out_shape=pltpu.VMEM((2, 1, 1, own, width), f32),
        in_specs=[pl.BlockSpec(memory_space=pltpu.HBM)] * 7,
        out_specs=vmem,
        scratch_shapes=[pltpu.VMEM(shape, kind) for shape, kind in buffers] + [
            sems((points // 256 + 6,)),
            sems((max(shells - 1, 1), shells, pieces)),
            sems((max(shells - 1, 1), shells, pieces)),
            sems((max(chips - 1, 1), shells, pieces)),
            sems((max(chips - 1, 1), shells, pieces)),
            sems((chips, shells, pieces)),
            sems((chips, shells, pieces)),
            sems((own // half,)),
            sems((own // half,)),
        ],
        compiler_params=pltpu.CompilerParams(
            collective_id=0, has_side_effects=True, vmem_limit_bytes=56 * 2**20
        ),
        cost_estimate=pl.CostEstimate(
            flops=2 * tile_rows * 2 * points * 2 * width + 4 * own * all_rows * 2 * width,
            bytes_accessed=8 * 2**20,
            transcendentals=0,
        ),
    )(left_basis, right_basis, point_weight, shell_index, green_table.T, pivot_rows, diag_inverse)


def solution(mesh):
    sizes = tuple(mesh.shape[name] for name in ("shell", "row", "col"))
    return jax.shard_map(
        functools.partial(body, sizes),
        mesh=mesh,
        in_specs=(
            P(None, "row", "shell"),
            P(None, "shell", "col"),
            P("shell"),
            P("shell"),
            P(),
            P(),
            P(),
        ),
        out_specs=P(None, "row", "shell", None, "col"),
        check_vma=False,
    )
```
